512 devices in a mesh: ctx: 64 (over z_lo, x, core), grp: 8 (over z_hi, y).
Axes of the slice: x: 4, y: 4, z: 16 (z_hi: 2, z_lo: 8; z = z_hi * 8 + z_lo), core: 2. Of those that a mesh axis runs over, the one named last changes fastest.
Arguments:
- queries: bfloat16 [8192, 4096], P('ctx', 'grp'), may hold values from -160 to 160
- key_vectors: bfloat16 [8192, 1024], P('ctx', 'grp'), may hold values from -6 to 6
- value_vectors: bfloat16 [8192, 1024], P('ctx', 'grp'), may hold values from -6 to 6
- grad_attn: bfloat16 [8192, 4096], P('ctx', 'grp'), may hold values from -6 to 6
- mamba_input: bfloat16 [8192, 16384], P('ctx', 'grp'), may hold values from -6 to 6
- step_sizes: bfloat16 [8192, 16384], P('ctx', 'grp'), may hold values from 0.0099487305 to 1
- decay_rates: float32 [16, 16384], P(None, 'grp'), may hold values from 0.0001 to 0.5
- write_coef: float32 [8192, 16], P('ctx'), may hold values from -1.5 to 1.5
- read_coef: float32 [8192, 16], P('ctx'), may hold values from -1.5 to 1.5
- grad_mamba: bfloat16 [8192, 16384], P('ctx', 'grp'), may hold values from -0.59765625 to 0.59765625
Outputs:
- grad_queries: bfloat16 [8192, 4096], P('ctx', 'grp')
- grad_keys: bfloat16 [8192, 1024], P('ctx', 'grp')
- grad_values: bfloat16 [8192, 1024], P('ctx', 'grp')
- grad_input: bfloat16 [8192, 16384], P('ctx', 'grp')
- grad_steps: bfloat16 [8192, 16384], P('ctx', 'grp')
- grad_write: float32 [8192, 16], P('ctx')
- grad_read: float32 [8192, 16], P('ctx')
The draws below stay inside these ranges and needn't reach their ends.
All inputs are finite; a program needn't handle non-finite values.
Results may differ from the reference program's by a relative error of at most 0.008.
Values may be sent and summed in bfloat16 or wider, within the bound.
A program may use at most 128 MiB of HBM per device.

```python
import math
import jax
import jax.numpy as jnp
from jax import lax

TOK_DEV = 128
HD = 128
QH_KV = 4
CH = 16384
NST = 16
SEQ = 8192
KVH = 8
QH = 32
N_CTX = 64


def shared_keys(key):
    raw_keys = jnp.clip(jax.random.normal(key, (SEQ, KVH * HD), jnp.float32), -6.0, 6.0)
    return raw_keys


def draw_key_vectors(key, part):
    raw_keys = shared_keys(key)
    return raw_keys.astype(jnp.bfloat16)


def draw_queries(key, part):
    key = jax.random.fold_in(key, 2)
    drawn = jnp.clip(jax.random.normal(key, (SEQ, QH * HD), jnp.float32), -6.0, 6.0)
    return drawn.astype(jnp.bfloat16)


def block_levels(rng, dims, pieces, low, largest):
    gain, own = 1.0, jax.random.fold_in(rng, 6)
    for position, blocks in pieces:
        steps = jnp.exp(jax.random.uniform(jax.random.fold_in(own, position), (blocks,), jnp.float32, low / len(pieces), largest / len(pieces)))
        gain = gain * jnp.repeat(steps, dims[position] // blocks).reshape([-1 if axis == position else 1 for axis in range(len(dims))])
    return gain


def normal_values(own_key, extent, deviation, bound, cuts=(), held_as=jnp.bfloat16):
    result = jax.random.normal(own_key, extent, jnp.float32) * deviation
    if len(cuts) > 0:
        result = block_levels(own_key, extent, cuts, -0.22, 0.18) * result
    return jnp.clip(result, min=-bound, max=bound).astype(held_as)


def setup_inputs(seed: int = 0) -> dict:
    seeds = jax.random.split(jax.random.key(seed), 11)
    return {
        "queries": draw_queries(jax.random.fold_in(seeds[10], 71), 0),
        "key_vectors": draw_key_vectors(jax.random.fold_in(seeds[10], 71), 0),
        "value_vectors": normal_values(seeds[2], (SEQ, KVH * HD), 1.0, 6.0, ((0, 64), (1, 8))),
        "grad_attn": normal_values(seeds[3], (SEQ, QH * HD), 1.0, 6.0, ((0, 64), (1, 8))),
        "mamba_input": normal_values(seeds[4], (SEQ, CH), 1.0, 6.0, ((0, 64), (1, 8))),
        "step_sizes": jnp.clip(jnp.exp(math.log(1.0) - 4.61031033 * jax.random.uniform(seeds[5], (SEQ, CH), jnp.float32) ** block_levels(seeds[5], (SEQ, CH), ((0, 64), (1, 8)), -0.2, 0.2)), 0.0099487305, 1.0).astype(jnp.bfloat16),
        "decay_rates": jnp.clip(jnp.exp(math.log(0.5) - 8.517193 * jax.random.uniform(seeds[6], (NST, CH), jnp.float32) ** block_levels(seeds[6], (NST, CH), ((1, 8),), -0.2, 0.2)), 0.0001, 0.5),
        "write_coef": normal_values(seeds[7], (SEQ, NST), 0.25, 1.5, ((0, 64),), jnp.float32),
        "read_coef": normal_values(seeds[8], (SEQ, NST), 0.25, 1.5, ((0, 64),), jnp.float32),
        "grad_mamba": normal_values(seeds[9], (SEQ, CH), 0.1, 0.59765625, ((0, 64), (1, 8))),
    }


def rounded(values):
    return lax.optimization_barrier(values.astype(jnp.bfloat16)).astype(jnp.float32)

def attention_grads(queries, key_vectors, value_vectors, grad_attn):
    highest = lax.Precision.HIGHEST
    score_scale = 1.0 / math.sqrt(HD)
    q_all = queries.astype(jnp.float32).reshape(SEQ, KVH, QH_KV, HD)
    g_all = grad_attn.astype(jnp.float32).reshape(SEQ, KVH, QH_KV, HD)
    k_all = key_vectors.astype(jnp.float32).reshape(SEQ, KVH, HD)
    v_all = value_vectors.astype(jnp.float32).reshape(SEQ, KVH, HD)
    span = math.gcd(SEQ, 256)
    count = SEQ // span

    def query_block(carried, blk_index):
        key_acc, value_acc = carried
        q_start = blk_index * span
        q_part = lax.dynamic_slice_in_dim(q_all, q_start, span, 0)
        g_part = lax.dynamic_slice_in_dim(g_all, q_start, span, 0)
        q_pos = q_start + jnp.arange(span, dtype=jnp.int32)

        def scores_of(key_index):
            k_start = key_index * span
            key_part = lax.dynamic_slice_in_dim(k_all, k_start, span, 0)
            value_part = lax.dynamic_slice_in_dim(v_all, k_start, span, 0)
            scores = jnp.einsum('tkgd,skd->kgts', q_part, key_part, precision=highest) * score_scale
            visible = (k_start + jnp.arange(span, dtype=jnp.int32))[None, :] <= q_pos[:, None]
            return (jnp.where(visible, scores, -jnp.inf), key_part, value_part, k_start)

        def forward(key_index, state_acc):
            run_max, run_sum, run_acc = state_acc
            scores, key_part, value_part, k_start = scores_of(key_index)
            new_max = jnp.maximum(run_max, lax.optimization_barrier(jnp.max(scores, axis=-1)))
            prob_full = jnp.exp(scores - new_max[..., None])
            shrink = jnp.exp(run_max - new_max)
            run_acc = run_acc * shrink[..., None] + jnp.einsum('kgts,skd->kgtd', prob_full, value_part, precision=highest)
            return (new_max, run_sum * shrink + lax.optimization_barrier(jnp.sum(prob_full, axis=-1)), run_acc)
        stat_shape = (KVH, QH_KV, span)
        start_state = (jnp.full(stat_shape, -jnp.inf, jnp.float32), jnp.zeros(stat_shape, jnp.float32), jnp.zeros(stat_shape + (HD,), jnp.float32))
        run_max, run_sum, run_acc = lax.fori_loop(0, blk_index + 1, forward, start_state)
        log_total = run_max + jnp.log(run_sum)
        attn_out = run_acc / run_sum[..., None]
        row_dot = jnp.einsum('tkgd,kgtd->kgt', g_part, attn_out, precision=highest)

        def backward(key_index, state_acc):
            query_acc, key_sum, value_sum = state_acc
            scores, key_part, value_part, k_start = scores_of(key_index)
            prob_full = jnp.exp(scores - log_total[..., None])
            weights = rounded(prob_full)
            prob_grad = jnp.einsum('tkgd,skd->kgts', g_part, value_part, precision=highest)
            score_grad = rounded(prob_full * (prob_grad - row_dot[..., None]) * score_scale)
            query_acc = query_acc + jnp.einsum('kgts,skd->tkgd', score_grad, key_part, precision=highest)
            key_add = jnp.einsum('kgts,tkgd->skd', score_grad, q_part, precision=highest)
            value_add = jnp.einsum('kgts,tkgd->skd', weights, g_part, precision=highest)
            key_sum = lax.dynamic_update_slice_in_dim(key_sum, lax.dynamic_slice_in_dim(key_sum, k_start, span, 0) + key_add, k_start, 0)
            value_sum = lax.dynamic_update_slice_in_dim(value_sum, lax.dynamic_slice_in_dim(value_sum, k_start, span, 0) + value_add, k_start, 0)
            return (query_acc, key_sum, value_sum)
        query_acc, key_acc, value_acc = lax.fori_loop(0, blk_index + 1, backward, (jnp.zeros((span, KVH, QH_KV, HD), jnp.float32), key_acc, value_acc))
        return ((key_acc, value_acc), query_acc.astype(jnp.bfloat16))
    zero_keys = jnp.zeros((SEQ, KVH, HD), jnp.float32)
    (key_acc, value_acc), query_blocks = lax.scan(query_block, (zero_keys, zero_keys), jnp.arange(count, dtype=jnp.int32))
    grad_queries = query_blocks.reshape(SEQ, QH * HD)
    grad_keys = key_acc.astype(jnp.bfloat16).reshape(SEQ, KVH * HD)
    grad_values = value_acc.astype(jnp.bfloat16).reshape(SEQ, KVH * HD)
    return (grad_queries, grad_keys, grad_values)

def scan_grads(mamba_input, step_sizes, decay_rates, write_coef, read_coef, grad_mamba):
    decay_rate = decay_rates.astype(jnp.float32)
    x_all = mamba_input.astype(jnp.float32).reshape(N_CTX, TOK_DEV, CH)
    step_all = step_sizes.astype(jnp.float32).reshape(N_CTX, TOK_DEV, CH)
    gy_all = grad_mamba.astype(jnp.float32).reshape(N_CTX, TOK_DEV, CH)
    write_all = write_coef.astype(jnp.float32).reshape(N_CTX, TOK_DEV, NST)
    read_all = read_coef.astype(jnp.float32).reshape(N_CTX, TOK_DEV, NST)

    def advance(state_now, packed):
        x_tok, step_tok, write_tok = packed
        decay_now = jnp.exp(-decay_rate * step_tok[None, :])
        return (decay_now * state_now + (step_tok * x_tok)[None, :] * write_tok[:, None], decay_now)

    def forward_tok(state_now, packed):
        new_state, decay_now = advance(state_now, packed)
        return (new_state, None)

    def forward_block(state_now, packed):
        end_state, unused = lax.scan(forward_tok, state_now, packed)
        return (end_state, state_now)
    zero_state = jnp.zeros((NST, CH), jnp.float32)
    unused, starts = lax.scan(forward_block, zero_state, (x_all, step_all, write_all))

    def backward_block(carried, packed):
        block_start, x_block, step_block, write_block, read_block, gy_block = packed

        def record(state_now, tok):
            new_state, decay_now = advance(state_now, tok)
            return (new_state, (new_state, decay_now))
        unused_end, (states, decays) = lax.scan(record, block_start, (x_block, step_block, write_block))
        prev_states = jnp.concatenate([block_start[None], states[:-1]], axis=0)

        def back_tok(grad_carry, tok):
            prev_state, state_now, decay_now, x_tok, step_tok, write_tok, read_tok, gy_tok = tok
            grad_now = read_tok[:, None] * gy_tok[None, :] + grad_carry
            grad_x = lax.optimization_barrier(jnp.sum(grad_now * write_tok[:, None], axis=0)) * step_tok
            grad_d = lax.optimization_barrier(jnp.sum(grad_now * (write_tok[:, None] * x_tok[None, :] - decay_rate * decay_now * prev_state), axis=0))
            grad_w = lax.optimization_barrier(jnp.sum(grad_now * (step_tok * x_tok)[None, :], axis=1))
            grad_r = lax.optimization_barrier(jnp.sum(state_now * gy_tok[None, :], axis=1))
            return (decay_now * grad_now, (grad_x, grad_d, grad_w, grad_r))
        return lax.scan(back_tok, carried, (prev_states, states, decays, x_block, step_block, write_block, read_block, gy_block), reverse=True)
    unused, (grad_x, grad_d, grad_w, grad_r) = lax.scan(backward_block, zero_state, (starts, x_all, step_all, write_all, read_all, gy_all), reverse=True)
    return (grad_x.reshape(SEQ, CH).astype(jnp.bfloat16), grad_d.reshape(SEQ, CH).astype(jnp.bfloat16), grad_w.reshape(SEQ, NST), grad_r.reshape(SEQ, NST))

def reference(queries, key_vectors, value_vectors, grad_attn, mamba_input, step_sizes, decay_rates, write_coef, read_coef, grad_mamba):
    grad_queries, grad_keys, grad_values = attention_grads(queries, key_vectors, value_vectors, grad_attn)
    grad_input, grad_steps, grad_write, grad_read = scan_grads(mamba_input, step_sizes, decay_rates, write_coef, read_coef, grad_mamba)
    return (grad_queries, grad_keys, grad_values, grad_input, grad_steps, grad_write, grad_read)
```

```python
import math

import jax
import jax.numpy as jnp
from jax import lax
from jax.experimental import pallas as pl
from jax.experimental.pallas import tpu as pltpu
from jax.sharding import PartitionSpec as P

MESH = pl.DeviceIdType.MESH
F32 = jnp.float32
BF16 = jnp.bfloat16
HD = 128
NST = 16
TOK = 128
PLANE = 8
NZ = 8
LOG2E = 1.4426950408889634
LN2 = 0.6931471805599453
SCALE = 1.0 / math.sqrt(HD)
NEG = -1e30
CW = 512
ROWS = 512


def dot(a, b, dims):
    return lax.dot_general(a, b, (dims, ((), ())), preferred_element_type=F32)


def kernel(
    q_ref, k_ref, v_ref, do_ref, x_ref, st_ref, rate_ref, b_ref, c_ref, gy_ref,
    dq_ref, dk_ref, dv_ref, gx_ref, gs_ref, gw_ref, gr_ref,
    qg, dog, kvg, stf, uf, gyf, bb, cb, tmp, ratel,
    ebuf, erecv, zmsg_up, zmsg_dn, zrecv_up, zrecv_dn, pre_f, pre_b, sin_f, sin_b, cbuf, crecv,
    mst, lst, rst, stat, lse, rdt,
    dqt, dqs, dqr, own, sib_s, sib_r, zs, zr,
    hs, avs, sg, sq, s1, s2, wacc, racc, wred, yrecv, hsum, hrecv,
    q_ss, q_rs, do_ss, do_rs, kz_ss, kz_rs, ks_ss, ks_rs, loc,
    ea_ss, ea_rs, eu_ss, eu_rs, ed_ss, ed_rs, ec_ss, ec_rs,
    sx_ss, sx_rs, dq_ss, dq_rs, si_ss, si_rs, zz_ss, zz_rs, y_ss, y_rs, hh_ss, hh_rs,
):
    channels = x_ref.shape[1]
    n_chunks = channels // CW
    slice_w = channels // PLANE
    c = lax.axis_index("ctx")
    g = lax.axis_index("grp")
    z = c // PLANE
    p = c % PLANE
    xx = p // 2
    core = p % 2
    sib = c + 1 - 2 * core
    base = z * PLANE
    y = g % 4
    gz = g - y

    def plane_peer(k):
        return (p + k) % PLANE

    def plane_from(k):
        return (p + PLANE - k) % PLANE

    def rcopy(src, dst, ss, rs, dev):
        return pltpu.make_async_remote_copy(
            src_ref=src, dst_ref=dst, send_sem=ss, recv_sem=rs, device_id=dev, device_id_type=MESH
        )

    bar = pltpu.get_barrier_semaphore()

    def greet(dev):
        pl.semaphore_signal(bar, inc=1, device_id=dev, device_id_type=MESH)

    for k in range(1, PLANE):
        greet({"ctx": base + plane_peer(k)})
    for k in range(1, NZ):
        greet({"ctx": ((z + k) % NZ) * PLANE + p})
    for k in range(1, 4):
        greet({"grp": gz + (y + k) % 4})
    greet({"grp": (g + 4) % 8})

    stf[...] = st_ref[...].astype(F32)
    uf[...] = stf[...] * x_ref[...].astype(F32)
    gyf[...] = gy_ref[...].astype(F32)
    ratel[...] = rate_ref[...] * (-LOG2E)
    tmp[...] = jnp.zeros_like(tmp)
    tmp[:, 0:NST] = b_ref[...]
    tmp[:, NST:2 * NST] = c_ref[...]
    bct = tmp[...].T[0:2 * NST, :]

    def spread(i, _):
        turned = pltpu.roll(bct, (TOK - 8 * i) % TOK, 1)
        for j in range(8):
            at = pl.ds(pl.multiple_of((8 * i + j) * NST, NST), NST)
            bb[at, :] = jnp.broadcast_to(turned[0:NST, j:j + 1], (NST, TOK))
            cb[at, :] = jnp.broadcast_to(turned[NST:2 * NST, j:j + 1], (NST, TOK))
        return 0

    lax.fori_loop(0, TOK // 8, spread, 0)

    kvg[z, pl.ds(pl.multiple_of(core * TOK, TOK), TOK), 0:HD] = k_ref[...]
    kvg[z, pl.ds(pl.multiple_of(core * TOK, TOK), TOK), HD:2 * HD] = v_ref[...]

    pl.semaphore_wait(bar, PLANE - 1 + NZ - 1 + 3 + 1)

    def q_copy(k, whole, gathered, ss, rs):
        dst = plane_peer(k)
        cols = pl.ds(pl.multiple_of((dst % 2) * 2 * HD, 2 * HD), 2 * HD)
        rows = pl.ds(pl.multiple_of(p * TOK, TOK), TOK)
        return rcopy(
            whole.at[:, cols], gathered.at[rows, :], ss.at[k], rs.at[k], {"ctx": base + dst}
        )

    def kv_copy(s, slot, to_sibling):
        rows = pl.ds(pl.multiple_of(core * TOK, TOK), TOK)
        part = kvg.at[slot, rows, :]
        if to_sibling:
            return rcopy(part, part, ks_ss.at[s], ks_rs.at[s], {"ctx": sib})
        return rcopy(part, part, kz_ss.at[s], kz_rs.at[s + 1], {"ctx": c + PLANE})

    def kv_step(s):
        slot = z - s

        @pl.when(slot >= 0)
        def _():
            @pl.when(s > 0)
            def _():
                part = kvg.at[slot, pl.ds(pl.multiple_of(core * TOK, TOK), TOK), :]
                rcopy(part, part, kz_ss.at[s], kz_rs.at[s], {"ctx": sib}).wait_recv()

            @pl.when(z < NZ - 1)
            def _():
                kv_copy(s, slot, False).start()

            kv_copy(s, slot, True).start()

    def kv_sib_wait(s):
        part = kvg.at[z - s, pl.ds(pl.multiple_of((1 - core) * TOK, TOK), TOK), :]
        rcopy(part, part, ks_ss.at[s], ks_rs.at[s], {"ctx": sib}).wait_recv()

    kv_step(jnp.int32(0))
    for k in range(1, PLANE):
        q_copy(k, q_ref, qg, q_ss, q_rs).start()
    for k in range(1, PLANE):
        q_copy(k, do_ref, dog, do_ss, do_rs).start()
    my_cols = pl.ds(pl.multiple_of(core * 2 * HD, 2 * HD), 2 * HD)
    my_rows = pl.ds(pl.multiple_of(p * TOK, TOK), TOK)
    loc_q = pltpu.make_async_copy(q_ref.at[:, my_cols], qg.at[my_rows, :], loc.at[0])
    loc_do = pltpu.make_async_copy(do_ref.at[:, my_cols], dog.at[my_rows, :], loc.at[1])
    loc_q.start()
    loc_do.start()

    def first_chunk(ch, _):
        lanes = pl.ds(pl.multiple_of(ch * CW, CW), CW)
        rt = ratel[:, lanes]

        def body(i, carry):
            h, pr, gg = carry
            for j in range(8):
                t = 8 * i + j
                at = pl.ds(pl.multiple_of(t * NST, NST), NST)
                bt = jnp.tile(bb[at, :], (1, CW // 128))
                ct = jnp.tile(cb[at, :], (1, CW // 128))
                a = jnp.exp2(rt * stf[pl.ds(t, 1), lanes])
                h = a * h + uf[pl.ds(t, 1), lanes] * bt
                pr = a * pr
                gg = gg + pr * (gyf[pl.ds(t, 1), lanes] * ct)
            return (h, pr, gg)

        zero = jnp.zeros((NST, CW), F32)
        h, pr, gg = lax.fori_loop(0, TOK // 8, body, (zero, jnp.ones((NST, CW), F32), zero))
        total = jnp.sum(stf[:, lanes], axis=0, keepdims=True)
        for half in range(CW // slice_w):
            to = ch * (CW // slice_w) + half
            cut = slice(half * slice_w, (half + 1) * slice_w)
            ebuf[to, 0:NST, :] = h[:, cut]
            ebuf[to, NST:2 * NST, :] = gg[:, cut]
            ebuf[to, 2 * NST:2 * NST + 8, :] = jnp.broadcast_to(total[:, cut], (8, slice_w))
        kv_step(ch + 1)
        return 0

    lax.fori_loop(0, n_chunks, first_chunk, 0)

    def e_copy(k):
        dst = plane_peer(k)
        return rcopy(ebuf.at[dst], erecv.at[p], ea_ss.at[k], ea_rs.at[k], {"ctx": base + dst})

    for k in range(1, PLANE):
        e_copy(k).start()
    own_e = pltpu.make_async_copy(ebuf.at[p], erecv.at[p], loc.at[2])
    own_e.start()

    mst[...] = jnp.full(mst.shape, NEG, F32)
    lst[...] = jnp.zeros_like(lst)
    rst[...] = jnp.zeros_like(rst)

    def tile_of(ch):
        head = ch // 2
        rows = pl.ds(pl.multiple_of((ch % 2) * ROWS, ROWS), ROWS)
        cols = pl.ds(pl.multiple_of(head * HD, HD), HD)
        lanes = pl.ds(pl.multiple_of(ch * ROWS, ROWS), ROWS)
        return rows, cols, lanes

    def seen(ch):
        key = xx * 2 * TOK + lax.broadcasted_iota(jnp.int32, (2 * TOK, ROWS), 0)
        query = (ch % 2) * ROWS + lax.broadcasted_iota(jnp.int32, (2 * TOK, ROWS), 1)
        return key <= query

    def attn_first(slot, diagonal):
        def body(ch, _):
            rows, cols, lanes = tile_of(ch)
            sc = dot(kvg[slot, :, 0:HD], qg[rows, cols], ((1,), (1,))) * (SCALE * LOG2E)
            if diagonal:
                sc = jnp.where(seen(ch), sc, NEG)
            sc = sc.reshape(2 * TOK // 8, 8, ROWS)
            dp = dot(kvg[slot, :, HD:2 * HD], dog[rows, cols], ((1,), (1,)))
            dp = dp.reshape(2 * TOK // 8, 8, ROWS)
            m_old = mst[:, lanes]
            m_new = jnp.maximum(m_old, jnp.max(sc, axis=0))
            shrink = jnp.exp2(m_old - m_new)
            pr = jnp.exp2(sc - m_new[None])
            mst[:, lanes] = m_new
            lst[:, lanes] = lst[:, lanes] * shrink + jnp.sum(pr, axis=0)
            rst[:, lanes] = rst[:, lanes] * shrink + jnp.sum(pr * dp, axis=0)
            return 0

        lax.fori_loop(0, 2 * 1024 // ROWS, body, 0)

    for k in range(1, PLANE):
        q_copy(k, q_ref, qg, q_ss, q_rs).wait()
        q_copy(k, do_ref, dog, do_ss, do_rs).wait()
    loc_q.wait()
    loc_do.wait()
    kv_sib_wait(jnp.int32(0))
    attn_first(z, True)

    for k in range(1, PLANE):
        e_copy(k).wait()
    own_e.wait()
    mine = pl.ds(pl.multiple_of(p * slice_w, slice_w), slice_w)
    rslice = ratel[:, mine]
    zero_s = jnp.zeros((NST, slice_w), F32)
    state = zero_s
    total = jnp.zeros((1, slice_w), F32)
    for j in range(PLANE):
        pre_f[j, 0:NST, :] = state
        pre_f[j, NST:2 * NST, :] = jnp.exp2(rslice * total)
        tj = erecv[j, 2 * NST:2 * NST + 1, :]
        state = jnp.exp2(rslice * tj) * state + erecv[j, 0:NST, :]
        total = total + tj
    plane_total = total
    zmsg_up[0:NST, :] = state
    zmsg_up[NST:NST + 8, :] = jnp.broadcast_to(plane_total, (8, slice_w))
    state = zero_s
    total = jnp.zeros((1, slice_w), F32)
    for j in range(PLANE - 1, -1, -1):
        pre_b[j, 0:NST, :] = state
        pre_b[j, NST:2 * NST, :] = jnp.exp2(rslice * total)
        tj = erecv[j, 2 * NST:2 * NST + 1, :]
        state = jnp.exp2(rslice * tj) * state + erecv[j, NST:2 * NST, :]
        total = total + tj
    zmsg_dn[0:NST, :] = state
    zmsg_dn[NST:NST + 8, :] = jnp.broadcast_to(plane_total, (8, slice_w))

    def up_copy(k):
        return rcopy(
            zmsg_up, zrecv_up.at[k], eu_ss.at[k], eu_rs.at[k], {"ctx": c + k * PLANE}
        )

    def dn_copy(k):
        return rcopy(
            zmsg_dn, zrecv_dn.at[k], ed_ss.at[k], ed_rs.at[k], {"ctx": c - k * PLANE}
        )

    for k in range(1, NZ):
        @pl.when(z + k < NZ)
        def _(k=k):
            up_copy(k).start()

        @pl.when(z - k >= 0)
        def _(k=k):
            dn_copy(k).start()

    def attn_step(s, _):
        @pl.when(s > n_chunks)
        def _():
            kv_step(s)

        kv_sib_wait(s)
        attn_first(z - s, False)
        return 0

    lax.fori_loop(1, z + 1, attn_step, 0)

    m8 = mst[...]
    m1 = jnp.max(m8, axis=0, keepdims=True)
    w8 = jnp.exp2(m8 - m1)
    l1 = jnp.sum(lst[...] * w8, axis=0, keepdims=True)
    r1 = jnp.sum(rst[...] * w8, axis=0, keepdims=True)
    n_rt = 2 * 1024 // 128
    for j in range(n_rt):
        cut = slice(j * 128, (j + 1) * 128)
        stat[0, j:j + 1, :] = m1[:, cut]
        stat[0, n_rt + j:n_rt + j + 1, :] = l1[:, cut]
        stat[0, 2 * n_rt + j:2 * n_rt + j + 1, :] = r1[:, cut]

    def stat_copy(k):
        dst = base + ((xx + k) % 4) * 2 + core
        return rcopy(stat.at[0], stat.at[k], sx_ss.at[k], sx_rs.at[k], {"ctx": dst})

    for k in range(1, 4):
        stat_copy(k).start()

    sin_f[...] = zero_s
    sin_b[...] = zero_s
    for k in range(NZ - 1, 0, -1):
        @pl.when(z - k >= 0)
        def _(k=k):
            rcopy(
                zmsg_up, zrecv_up.at[k], eu_ss.at[k], eu_rs.at[k], {"ctx": sib}
            ).wait_recv()
            dec = jnp.exp2(rslice * zrecv_up[k, NST:NST + 1, :])
            sin_f[...] = dec * sin_f[...] + zrecv_up[k, 0:NST, :]

        @pl.when(z + k < NZ)
        def _(k=k):
            rcopy(
                zmsg_dn, zrecv_dn.at[k], ed_ss.at[k], ed_rs.at[k], {"ctx": sib}
            ).wait_recv()
            dec = jnp.exp2(rslice * zrecv_dn[k, NST:NST + 1, :])
            sin_b[...] = dec * sin_b[...] + zrecv_dn[k, 0:NST, :]
    for j in range(PLANE):
        cbuf[j, 0:NST, :] = pre_f[j, 0:NST, :] + pre_f[j, NST:2 * NST, :] * sin_f[...]
        cbuf[j, NST:2 * NST, :] = pre_b[j, 0:NST, :] + pre_b[j, NST:2 * NST, :] * sin_b[...]

    def c_copy(k):
        dst = plane_peer(k)
        return rcopy(cbuf.at[dst], crecv.at[p], ec_ss.at[k], ec_rs.at[k], {"ctx": base + dst})

    for k in range(1, PLANE):
        c_copy(k).start()
    own_c = pltpu.make_async_copy(cbuf.at[p], crecv.at[p], loc.at[3])
    own_c.start()

    for k in range(1, 4):
        stat_copy(k).wait()
    m4 = [stat[k, 0:n_rt, :] for k in range(4)]
    m_all = jnp.maximum(jnp.maximum(m4[0], m4[1]), jnp.maximum(m4[2], m4[3]))
    l_all = jnp.zeros((n_rt, 128), F32)
    r_all = jnp.zeros((n_rt, 128), F32)
    for k in range(4):
        w = jnp.exp2(m4[k] - m_all)
        l_all = l_all + w * stat[k, n_rt:2 * n_rt, :]
        r_all = r_all + w * stat[k, 2 * n_rt:3 * n_rt, :]
    lse_t = m_all + jnp.log2(l_all)
    rd_t = r_all / l_all
    for j in range(n_rt):
        cut = slice(j * 128, (j + 1) * 128)
        lse[:, cut] = jnp.broadcast_to(lse_t[j:j + 1, :], (8, 128))
        rdt[:, cut] = jnp.broadcast_to(rd_t[j:j + 1, :], (8, 128))

    dqt[...] = jnp.zeros_like(dqt)

    def attn_second(s, slot, diagonal):
        keys_t = kvg[slot, :, 0:HD].T

        def body(ch, carry):
            dk, dv = carry
            rows, cols, lanes = tile_of(ch)
            keys = kvg[slot, :, 0:HD]
            sc = dot(keys, qg[rows, cols], ((1,), (1,))) * (SCALE * LOG2E)
            pr = jnp.exp2(sc.reshape(2 * TOK // 8, 8, ROWS) - lse[:, lanes][None])
            if diagonal:
                pr = jnp.where(seen(ch).reshape(pr.shape), pr, 0.0)
            dp = dot(kvg[slot, :, HD:2 * HD], dog[rows, cols], ((1,), (1,)))
            ds = pr * (dp.reshape(pr.shape) - rdt[:, lanes][None])
            pb = pr.reshape(2 * TOK, ROWS).astype(BF16)
            db = ds.reshape(2 * TOK, ROWS).astype(BF16)
            dv = dv + dot(pb, dog[rows, cols], ((1,), (0,)))
            dk = dk + dot(db, qg[rows, cols], ((1,), (0,)))
            head = pl.ds(pl.multiple_of((ch // 2) * HD, HD), HD)
            dqt[head, rows] += dot(keys_t, db, ((1,), (0,)))
            return dk, dv

        zero = jnp.zeros((2 * TOK, HD), F32)
        dk, dv = lax.fori_loop(0, 2 * 1024 // ROWS, body, (zero, zero))
        dk = dk * SCALE
        first = core == 0
        own[s, :, 0:HD] = jnp.where(first, dk[0:TOK], dk[TOK:])
        own[s, :, HD:2 * HD] = jnp.where(first, dv[0:TOK], dv[TOK:])
        sib_s[s, :, 0:HD] = jnp.where(first, dk[TOK:], dk[0:TOK])
        sib_s[s, :, HD:2 * HD] = jnp.where(first, dv[TOK:], dv[0:TOK])
        sib_copy(s).start()

    def sib_copy(s):
        return rcopy(sib_s.at[s], sib_r.at[s], si_ss.at[s], si_rs.at[s], {"ctx": sib})

    def z_copy(s):
        return rcopy(
            zs.at[s], zr.at[s], zz_ss.at[s], zz_rs.at[s], {"ctx": c - s * PLANE}
        )

    def hand_down(s):
        sib_copy(s).wait()
        zs[s] = (own[s] + sib_r[s]).astype(BF16)
        z_copy(s).start()

    def second_step(i, _):
        s = z - i
        attn_second(s, z - s, False)

        @pl.when(i > 0)
        def _():
            hand_down(s + 1)

        return 0

    lax.fori_loop(0, z, second_step, 0)
    attn_second(jnp.int32(0), z, True)

    @pl.when(z > 0)
    def _():
        hand_down(jnp.int32(1))

    dqs[...] = (dqt[...] * SCALE).astype(BF16)

    def dq_copy(k):
        dst = plane_peer(k)
        cols = pl.ds(pl.multiple_of(dst * TOK, TOK), TOK)
        return rcopy(
            dqs.at[:, cols], dqr.at[p], dq_ss.at[k], dq_rs.at[k], {"ctx": base + dst}
        )

    for k in range(1, PLANE):
        dq_copy(k).start()
    own_dq = pltpu.make_async_copy(
        dqs.at[:, pl.ds(pl.multiple_of(p * TOK, TOK), TOK)], dqr.at[p], loc.at[4]
    )
    own_dq.start()
    sib_copy(jnp.int32(0)).wait()

    for k in range(1, PLANE):
        c_copy(k).wait()
    own_c.wait()

    def second_chunk(ch, _):
        lanes = pl.ds(pl.multiple_of(ch * CW, CW), CW)
        rt = ratel[:, lanes]
        per = CW // slice_w
        h_in = jnp.concatenate([crecv[ch * per + i, 0:NST, :] for i in range(per)], axis=1)
        g_in = jnp.concatenate([crecv[ch * per + i, NST:2 * NST, :] for i in range(per)], axis=1)
        hs[0:NST, :] = h_in

        def forward(i, h):
            for j in range(8):
                t = 8 * i + j
                at = pl.ds(pl.multiple_of(t * NST, NST), NST)
                bt = jnp.tile(bb[at, :], (1, CW // 128))
                a = jnp.exp2(rt * stf[pl.ds(t, 1), lanes])
                h = a * h + uf[pl.ds(t, 1), lanes] * bt
                avs[at, :] = a
                hs[pl.ds(pl.multiple_of((t + 1) * NST, NST), NST), :] = h
            return h

        lax.fori_loop(0, TOK // 8, forward, h_in)

        def folded(v):
            out = v[:, 0:128]
            for i in range(1, CW // 128):
                out = out + v[:, i * 128:(i + 1) * 128]
            return out

        def backward(i, carry):
            lo = TOK // 8 - 1 - i
            for j in range(7, -1, -1):
                t = 8 * lo + j
                at = pl.ds(pl.multiple_of(t * NST, NST), NST)
                bt = jnp.tile(bb[at, :], (1, CW // 128))
                ct = jnp.tile(cb[at, :], (1, CW // 128))
                gyt = gyf[pl.ds(t, 1), lanes]
                gn = ct * gyt + carry
                carry = avs[at, :] * gn
                qv = carry * rt * hs[at, :]
                gb = gn * bt
                for v in range(CW // 128):
                    cut = slice(v * 128, (v + 1) * 128)
                    sg[v, j * 8:(j + 1) * 8, :] = gb[0:8, cut] + gb[8:16, cut]
                    sq[v, j * 8:(j + 1) * 8, :] = qv[0:8, cut] + qv[8:16, cut]
                wacc[at, :] += folded(gn * uf[pl.ds(t, 1), lanes])
                racc[at, :] += folded(
                    hs[pl.ds(pl.multiple_of((t + 1) * NST, NST), NST), :] * gyt
                )
            rows = pl.ds(pl.multiple_of(8 * lo, 8), 8)
            for v in range(CW // 128):
                cut = slice(v * 128, (v + 1) * 128)
                a1 = sg[v, pl.ds(0, 8, stride=8), :]
                a2 = sq[v, pl.ds(0, 8, stride=8), :]
                for n in range(1, 8):
                    a1 = a1 + sg[v, pl.ds(n, 8, stride=8), :]
                    a2 = a2 + sq[v, pl.ds(n, 8, stride=8), :]
                s1[rows, cut] = a1
                s2[rows, cut] = a2
            return carry

        lax.fori_loop(0, TOK // 8, backward, g_in)
        gx_ref[:, lanes] = (s1[...] * stf[:, lanes]).astype(BF16)
        gs_ref[:, lanes] = (
            s1[...] * x_ref[:, lanes].astype(F32) + LN2 * s2[...]
        ).astype(BF16)
        return 0

    wacc[...] = jnp.zeros_like(wacc)
    racc[...] = jnp.zeros_like(racc)
    lax.fori_loop(0, n_chunks, second_chunk, 0)

    def lanes_sum(i, _):
        at = pl.ds(pl.multiple_of(i * 8 * NST, 8 * NST), 8 * NST)
        row = lax.broadcasted_iota(jnp.int32, (8 * NST, 128), 0) % NST
        lane = lax.broadcasted_iota(jnp.int32, (8 * NST, 128), 1)
        ws = jnp.sum(wacc[at, :], axis=1, keepdims=True)
        rs = jnp.sum(racc[at, :], axis=1, keepdims=True)
        both = jnp.where(lane == row, ws, 0.0) + jnp.where(lane == row + NST, rs, 0.0)
        tmp[pl.ds(pl.multiple_of(i * 8, 8), 8), :] = jnp.sum(both.reshape(8, NST, 128), axis=1)
        return 0

    lax.fori_loop(0, TOK // 8, lanes_sum, 0)
    wred[...] = tmp[...].T[0:2 * NST, :]

    def y_copy(k):
        return rcopy(wred, yrecv.at[k], y_ss.at[k], y_rs.at[k], {"grp": gz + (y + k) % 4})

    for k in range(1, 4):
        y_copy(k).start()

    for k in range(1, PLANE):
        dq_copy(k).wait()
    own_dq.wait()
    for cc in range(2):
        tot = dqr[cc].astype(F32)
        for i in range(1, 4):
            tot = tot + dqr[2 * i + cc].astype(F32)
        for h in range(2):
            col = (cc * 2 + h) * HD
            dq_ref[:, col:col + HD] = tot[h * HD:(h + 1) * HD, :].T.astype(BF16)

    for k in range(1, 4):
        y_copy(k).wait()
    hsum[...] = wred[...] + yrecv[1] + yrecv[2] + yrecv[3]
    h_copy = rcopy(hsum, hrecv, hh_ss, hh_rs, {"grp": (g + 4) % 8})
    h_copy.start()

    own[0] = own[0] + sib_r[0]
    for k in range(1, NZ):
        @pl.when(z + k < NZ)
        def _(k=k):
            rcopy(zs.at[k], zr.at[k], zz_ss.at[k], zz_rs.at[k], {"ctx": sib}).wait_recv()
            own[0] = own[0] + zr[k].astype(F32)
    dk_ref[...] = own[0, :, 0:HD].astype(BF16)
    dv_ref[...] = own[0, :, HD:2 * HD].astype(BF16)

    h_copy.wait()
    tmp[0:2 * NST, :] = hsum[...] + hrecv[...]
    back = tmp[...].T
    gw_ref[...] = back[:, 0:NST]
    gr_ref[...] = back[:, NST:2 * NST]

    for k in range(1, NZ):
        @pl.when(z + k < NZ)
        def _(k=k):
            up_copy(k).wait_send()

        @pl.when(z - k >= 0)
        def _(k=k):
            dn_copy(k).wait_send()
            z_copy(k).wait_send()
    for s in range(NZ):
        @pl.when(z - s >= 0)
        def _(s=s):
            kv_copy(s, z - s, True).wait_send()

            @pl.when(z < NZ - 1)
            def _():
                kv_copy(s, z - s, False).wait_send()


def on_device(
    queries, key_vectors, value_vectors, grad_attn, mamba_input, step_sizes, decay_rates,
    write_coef, read_coef, grad_mamba,
):
    channels = mamba_input.shape[1]
    slice_w = channels // PLANE
    vmem = pltpu.VMEM
    dma = pltpu.SemaphoreType.DMA
    scratch = [
        vmem((1024, 256), BF16), vmem((1024, 256), BF16), vmem((NZ, 256, 256), BF16),
        vmem((TOK, channels), F32), vmem((TOK, channels), F32), vmem((TOK, channels), F32),
        vmem((TOK * NST, 128), F32), vmem((TOK * NST, 128), F32), vmem((128, 128), F32),
        vmem((NST, channels), F32),
        vmem((PLANE, 40, slice_w), F32), vmem((PLANE, 40, slice_w), F32),
        vmem((24, slice_w), F32), vmem((24, slice_w), F32),
        vmem((NZ, 24, slice_w), F32), vmem((NZ, 24, slice_w), F32),
        vmem((PLANE, 32, slice_w), F32), vmem((PLANE, 32, slice_w), F32),
        vmem((NST, slice_w), F32), vmem((NST, slice_w), F32),
        vmem((PLANE, 32, slice_w), F32), vmem((PLANE, 32, slice_w), F32),
        vmem((8, 2048), F32), vmem((8, 2048), F32), vmem((8, 2048), F32),
        vmem((4, 48, 128), F32), vmem((8, 2048), F32), vmem((8, 2048), F32),
        vmem((256, 1024), F32), vmem((256, 1024), BF16), vmem((PLANE, 256, 128), BF16),
        vmem((NZ, 128, 256), F32), vmem((NZ, 128, 256), F32), vmem((NZ, 128, 256), F32),
        vmem((NZ, 128, 256), BF16), vmem((NZ, 128, 256), BF16),
        vmem(((TOK + 1) * NST, CW), F32), vmem((TOK * NST, CW), F32),
        vmem((CW // 128, 64, 128), F32), vmem((CW // 128, 64, 128), F32), vmem((TOK, CW), F32), vmem((TOK, CW), F32),
        vmem((TOK * NST, 128), F32), vmem((TOK * NST, 128), F32),
        vmem((32, 128), F32), vmem((4, 32, 128), F32), vmem((32, 128), F32), vmem((32, 128), F32),
        dma((8,)), dma((8,)), dma((8,)), dma((8,)), dma((8,)), dma((8,)), dma((8,)), dma((8,)),
        dma((8,)),
        dma((8,)), dma((8,)), dma((8,)), dma((8,)), dma((8,)), dma((8,)), dma((8,)), dma((8,)),
        dma((4,)), dma((4,)), dma((8,)), dma((8,)), dma((8,)), dma((8,)), dma((8,)), dma((8,)),
        dma((4,)), dma((4,)), dma, dma,
    ]
    outs = (
        jax.ShapeDtypeStruct(queries.shape, BF16),
        jax.ShapeDtypeStruct(key_vectors.shape, BF16),
        jax.ShapeDtypeStruct(value_vectors.shape, BF16),
        jax.ShapeDtypeStruct(mamba_input.shape, BF16),
        jax.ShapeDtypeStruct(step_sizes.shape, BF16),
        jax.ShapeDtypeStruct(write_coef.shape, F32),
        jax.ShapeDtypeStruct(read_coef.shape, F32),
    )
    return pl.pallas_call(
        kernel,
        out_shape=outs,
        in_specs=[pl.BlockSpec(memory_space=pltpu.VMEM)] * 10,
        out_specs=(pl.BlockSpec(memory_space=pltpu.VMEM),) * 7,
        scratch_shapes=scratch,
        compiler_params=pltpu.CompilerParams(
            collective_id=0, has_side_effects=True, vmem_limit_bytes=56 * 2**20
        ),
    )(
        queries, key_vectors, value_vectors, grad_attn, mamba_input, step_sizes, decay_rates,
        write_coef, read_coef, grad_mamba,
    )


def solution(mesh):
    both = P("ctx", "grp")
    rows = P("ctx", None)
    return jax.shard_map(
        on_device,
        mesh=mesh,
        in_specs=(both,) * 6 + (P(None, "grp"), rows, rows, both),
        out_specs=(both,) * 5 + (rows, rows),
        check_vma=False,
    )
```

```python
import math

import jax
import jax.numpy as jnp
from jax import lax
from jax.experimental import pallas as pl
from jax.experimental.pallas import tpu as pltpu
from jax.sharding import PartitionSpec as P

MESH = pl.DeviceIdType.MESH
F32 = jnp.float32
BF16 = jnp.bfloat16
HD = 128
NST = 16
TOK = 128
PLANE = 8
NZ = 8
LOG2E = 1.4426950408889634
LN2 = 0.6931471805599453
SCALE = 1.0 / math.sqrt(HD)
NEG = -1e30
CW = 512
ROWS = 512
KV_ROWS = 32


def dot(a, b, dims):
    return lax.dot_general(a, b, (dims, ((), ())), preferred_element_type=F32)


def kernel(
    q_ref, k_ref, v_ref, do_ref, x_ref, st_ref, rate_ref, b_ref, c_ref, gy_ref,
    dq_ref, dk_ref, dv_ref, gx_ref, gs_ref, gw_ref, gr_ref,
    xb, stb, gyb, rates, bct, spr, qg, dog, kvg, stf, uf, gyf, bb, cb, tmp, ratel,
    ebuf, erecv, zmsg_up, zmsg_dn, zrecv_up, zrecv_dn, pre_f, pre_b, sin_f, sin_b, cbuf, crecv,
    mst, lst, rst, stat, lse, rdt,
    dqt, dqs, dqr, own, sib_s, sib_r, zs, zr,
    hs, avs, cum, sg, sq, s1, s2, wacc, racc, wred, yrecv, hsum, hrecv,
    q_ss, q_rs, do_ss, do_rs, kz_ss, kz_rs, ks_ss, ks_rs, loc,
    ea_ss, ea_rs, eu_ss, eu_rs, ed_ss, ed_rs, ec_ss, ec_rs,
    sx_ss, sx_rs, dq_ss, dq_rs, si_ss, si_rs, zz_ss, zz_rs, y_ss, y_rs, hh_ss, hh_rs, ld,
    etot, ertot, ztot, ztr_up, ztr_dn, et_ss, et_rs, ut_ss, ut_rs, dt_ss, dt_rs,
):
    channels = xb.shape[1]
    n_chunks = channels // CW
    slice_w = channels // PLANE
    c = lax.axis_index("ctx")
    g = lax.axis_index("grp")
    z = c // PLANE
    p = c % PLANE
    xx = p // 2
    core = p % 2
    sib = c + 1 - 2 * core
    base = z * PLANE
    y = g % 4
    gz = g - y

    def plane_peer(k):
        return (p + k) % PLANE

    def plane_from(k):
        return (p + PLANE - k) % PLANE

    def rcopy(src, dst, ss, rs, dev):
        return pltpu.make_async_remote_copy(
            src_ref=src, dst_ref=dst, send_sem=ss, recv_sem=rs, device_id=dev, device_id_type=MESH
        )

    bar = pltpu.get_barrier_semaphore()

    def greet(dev):
        pl.semaphore_signal(bar, inc=1, device_id=dev, device_id_type=MESH)

    greet({"grp": (g + 4) % 8})
    for k in (4, 3, 5, 2, 6, 1, 7):
        greet({"ctx": ((z + k) % NZ) * PLANE + p})
    for k in range(1, 4):
        greet({"grp": gz + (y + k) % 4})
    for k in range(1, PLANE):
        greet({"ctx": base + plane_peer(k)})

    key_rows = pl.ds(pl.multiple_of(core * TOK, TOK), TOK)
    loads = [
        pltpu.make_async_copy(src, dst, ld.at[i])
        for i, (src, dst) in enumerate((
            (st_ref, stb), (x_ref, xb), (gy_ref, gyb), (rate_ref, rates),
            (b_ref, bct.at[0:NST, :]), (c_ref, bct.at[NST:2 * NST, :]),
            (k_ref, kvg.at[z, key_rows, 0:HD]), (v_ref, kvg.at[z, key_rows, HD:2 * HD]),
        ))
    ]
    for load in loads:
        load.start()

    loads[4].wait()
    loads[5].wait()
    exact = bct[...]
    tmp[...] = jnp.zeros_like(tmp)
    for i in range(3):
        piece = exact.astype(BF16).astype(F32)
        tmp[2 * NST * i:2 * NST * (i + 1), :] = piece
        exact = exact - piece
    spr[...] = tmp[...].T
    own_state = (
        lax.broadcasted_iota(jnp.int32, (NST, 128), 1) % NST
        == lax.broadcasted_iota(jnp.int32, (NST, 128), 0)
    )
    pick = jnp.where(
        (lax.broadcasted_iota(jnp.int32, (128, 256), 0) // NST) % 2
        == lax.broadcasted_iota(jnp.int32, (128, 256), 1) // 128,
        1.0, 0.0,
    ).astype(BF16)

    def spread(i, _):
        rows = [
            jnp.where(own_state, jnp.broadcast_to(spr[pl.ds(8 * i + j, 1), :], (NST, 128)), 0.0)
            for j in range(8)
        ]
        both = dot(jnp.concatenate(rows, axis=0).astype(BF16), pick, ((1,), (0,)))
        at = pl.ds(pl.multiple_of(8 * i * NST, 8 * NST), 8 * NST)
        bb[at, :] = both[:, 0:128]
        cb[at, :] = both[:, 128:256]
        return 0

    lax.fori_loop(0, TOK // 8, spread, 0, unroll=4)
    for load in loads[0:4]:
        load.wait()
    stf[...] = stb[...].astype(F32)
    uf[...] = stf[...] * xb[...].astype(F32)
    gyf[...] = gyb[...].astype(F32)
    ratel[...] = rates[...] * (-LOG2E)
    def put_total(ref, row):
        for i in range(slice_w // 128):
            ref[i:i + 1, :] = row[:, i * 128:(i + 1) * 128]

    def get_total(ref):
        return jnp.concatenate([ref[i:i + 1, :] for i in range(slice_w // 128)], axis=1)

    earlier = jnp.where(
        lax.broadcasted_iota(jnp.int32, (TOK + 8, TOK), 0)
        > lax.broadcasted_iota(jnp.int32, (TOK + 8, TOK), 1),
        1.0, 0.0,
    ).astype(BF16)

    def first_chunk(ch, _):
        lanes = pl.ds(pl.multiple_of(ch * CW, CW), CW)
        rt = ratel[:, lanes]

        def body(i, carry):
            h, pr, gg = carry
            for j in range(8):
                t = 8 * i + j
                at = pl.ds(pl.multiple_of(t * NST, NST), NST)
                bt = jnp.tile(bb[at, :], (1, CW // 128))
                ct = jnp.tile(cb[at, :], (1, CW // 128))
                a = jnp.exp2(rt * stf[pl.ds(t, 1), lanes])
                avs[at, lanes] = a
                h = a * h + uf[pl.ds(t, 1), lanes] * bt
                hs[pl.ds(pl.multiple_of((t + 1) * NST, NST), NST), lanes] = h
                pr = a * pr
                gg = gg + pr * (gyf[pl.ds(t, 1), lanes] * ct)
            return (h, pr, gg)

        zero = jnp.zeros((NST, CW), F32)
        hs[0:NST, lanes] = zero
        h, pr, gg = lax.fori_loop(0, TOK // 8, body, (zero, jnp.ones((NST, CW), F32), zero))
        before = dot(earlier, stb[:, lanes], ((1,), (0,)))
        total = before[TOK:TOK + 1, :]
        cum[:, lanes] = before
        for half in range(CW // slice_w):
            to = ch * (CW // slice_w) + half
            cut = slice(half * slice_w, (half + 1) * slice_w)
            ebuf[to, 0:NST, :] = h[:, cut].astype(BF16)
            ebuf[to, NST:2 * NST, :] = gg[:, cut].astype(BF16)
            put_total(etot.at[to], total[:, cut])
        return 0

    lax.fori_loop(0, 1, first_chunk, 0)
    loads[6].wait()
    loads[7].wait()

    pl.semaphore_wait(bar, PLANE - 1 + NZ - 1 + 3 + 1)

    def q_copy(k, whole, gathered, ss, rs):
        dst = plane_peer(k)
        cols = pl.ds(pl.multiple_of((dst % 2) * 2 * HD, 2 * HD), 2 * HD)
        rows = pl.ds(pl.multiple_of(p * TOK, TOK), TOK)
        return rcopy(
            whole.at[:, cols], gathered.at[rows, :], ss.at[k], rs.at[k], {"ctx": base + dst}
        )

    def kv_part(slot, piece):
        at = core * TOK + piece * KV_ROWS
        return kvg.at[slot, pl.ds(pl.multiple_of(at, KV_ROWS), KV_ROWS), :]

    def kv_up(s, slot, piece):
        part = kv_part(slot, piece)
        return rcopy(part, part, kz_ss.at[s, piece], kz_rs.at[s + 1, piece], {"ctx": c + PLANE})

    def kv_over(s, slot):
        part = kvg.at[slot, pl.ds(pl.multiple_of(core * TOK, TOK), TOK), :]
        return rcopy(part, part, ks_ss.at[s], ks_rs.at[s], {"ctx": sib})

    def kv_step(s):
        slot = z - s

        @pl.when(slot >= 0)
        def _():
            for piece in range(TOK // KV_ROWS):
                @pl.when(s > 0)
                def _():
                    part = kv_part(slot, piece)
                    rcopy(
                        part, part, kz_ss.at[s, piece], kz_rs.at[s, piece], {"ctx": sib}
                    ).wait_recv()

                @pl.when(z < NZ - 1)
                def _():
                    kv_up(s, slot, piece).start()

            kv_over(s, slot).start()

    def kv_sib_wait(s):
        part = kvg.at[z - s, pl.ds(pl.multiple_of((1 - core) * TOK, TOK), TOK), :]
        rcopy(part, part, ks_ss.at[s], ks_rs.at[s], {"ctx": sib}).wait_recv()

    kv_step(jnp.int32(0))
    for k in range(1, PLANE):
        q_copy(k, q_ref, qg, q_ss, q_rs).start()
    my_cols = pl.ds(pl.multiple_of(core * 2 * HD, 2 * HD), 2 * HD)
    my_rows = pl.ds(pl.multiple_of(p * TOK, TOK), TOK)
    loc_q = pltpu.make_async_copy(q_ref.at[:, my_cols], qg.at[my_rows, :], loc.at[0])
    loc_do = pltpu.make_async_copy(do_ref.at[:, my_cols], dog.at[my_rows, :], loc.at[1])
    loc_q.start()
    loc_do.start()

    def first_step(ch, _):
        first_chunk(ch, 0)

        @pl.when(ch >= 2)
        def _():
            kv_step(ch - 1)

        return 0

    lax.fori_loop(1, n_chunks, first_step, 0)

    def e_copy(k):
        dst = plane_peer(k)
        return rcopy(ebuf.at[dst], erecv.at[p], ea_ss.at[k], ea_rs.at[k], {"ctx": base + dst})

    def et_copy(k):
        dst = plane_peer(k)
        return rcopy(etot.at[dst], ertot.at[p], et_ss.at[k], et_rs.at[k], {"ctx": base + dst})

    for k in range(1, PLANE):
        e_copy(k).start()
        et_copy(k).start()
    for k in range(1, PLANE):
        q_copy(k, do_ref, dog, do_ss, do_rs).start()
    erecv[p] = ebuf[p]
    ertot[p] = etot[p]

    mst[...] = jnp.full(mst.shape, NEG, F32)
    lst[...] = jnp.zeros_like(lst)
    rst[...] = jnp.zeros_like(rst)

    def tile_of(ch):
        head = ch // (1024 // ROWS)
        rows = pl.ds(pl.multiple_of((ch % (1024 // ROWS)) * ROWS, ROWS), ROWS)
        cols = pl.ds(pl.multiple_of(head * HD, HD), HD)
        lanes = pl.ds(pl.multiple_of(ch * ROWS, ROWS), ROWS)
        return rows, cols, lanes

    def seen(ch):
        key = xx * 2 * TOK + lax.broadcasted_iota(jnp.int32, (2 * TOK, ROWS), 0)
        query = (ch % (1024 // ROWS)) * ROWS + lax.broadcasted_iota(jnp.int32, (2 * TOK, ROWS), 1)
        return key <= query

    def attn_first(slot, diagonal):
        def body(ch, _):
            rows, cols, lanes = tile_of(ch)
            sc = dot(kvg[slot, :, 0:HD], qg[rows, cols], ((1,), (1,))) * (SCALE * LOG2E)
            if diagonal:
                sc = jnp.where(seen(ch), sc, NEG)
            sc = sc.reshape(2 * TOK // 8, 8, ROWS)
            dp = dot(kvg[slot, :, HD:2 * HD], dog[rows, cols], ((1,), (1,)))
            dp = dp.reshape(2 * TOK // 8, 8, ROWS)
            m_old = mst[:, lanes]
            m_new = jnp.maximum(m_old, jnp.max(sc, axis=0))
            shrink = jnp.exp2(m_old - m_new)
            pr = jnp.exp2(sc - m_new[None])
            mst[:, lanes] = m_new
            lst[:, lanes] = lst[:, lanes] * shrink + jnp.sum(pr, axis=0)
            rst[:, lanes] = rst[:, lanes] * shrink + jnp.sum(pr * dp, axis=0)
            return 0

        lax.fori_loop(0, 2 * 1024 // ROWS, body, 0, unroll=True)

    kv_step(jnp.int32(3))

    for k in range(1, PLANE):
        e_copy(k).wait()
        et_copy(k).wait()
    mine = pl.ds(pl.multiple_of(p * slice_w, slice_w), slice_w)
    rslice = ratel[:, mine]
    zero_s = jnp.zeros((NST, slice_w), F32)
    state = zero_s
    total = jnp.zeros((1, slice_w), F32)
    for j in range(PLANE):
        pre_f[j, 0:NST, :] = state
        pre_f[j, NST:2 * NST, :] = jnp.exp2(rslice * total)
        tj = get_total(ertot.at[j])
        state = jnp.exp2(rslice * tj) * state + erecv[j, 0:NST, :].astype(F32)
        total = total + tj
    plane_total = total
    zmsg_up[...] = state.astype(BF16)
    put_total(ztot, plane_total)
    state = zero_s
    total = jnp.zeros((1, slice_w), F32)
    for j in range(PLANE - 1, -1, -1):
        pre_b[j, 0:NST, :] = state
        pre_b[j, NST:2 * NST, :] = jnp.exp2(rslice * total)
        tj = get_total(ertot.at[j])
        state = jnp.exp2(rslice * tj) * state + erecv[j, NST:2 * NST, :].astype(F32)
        total = total + tj
    zmsg_dn[...] = state.astype(BF16)

    def up_copy(k):
        return rcopy(
            zmsg_up, zrecv_up.at[k], eu_ss.at[k], eu_rs.at[k], {"ctx": c + k * PLANE}
        )

    def dn_copy(k):
        return rcopy(
            zmsg_dn, zrecv_dn.at[k], ed_ss.at[k], ed_rs.at[k], {"ctx": c - k * PLANE}
        )

    def upt_copy(k):
        return rcopy(ztot, ztr_up.at[k], ut_ss.at[k], ut_rs.at[k], {"ctx": c + k * PLANE})

    def dnt_copy(k):
        return rcopy(ztot, ztr_dn.at[k], dt_ss.at[k], dt_rs.at[k], {"ctx": c - k * PLANE})

    for k in range(1, NZ):
        @pl.when(z + k < NZ)
        def _(k=k):
            upt_copy(k).start()
            up_copy(k).start()

        @pl.when(z - k >= 0)
        def _(k=k):
            dnt_copy(k).start()
            dn_copy(k).start()

    kv_step(jnp.int32(4))
    for k in range(1, PLANE):
        q_copy(k, q_ref, qg, q_ss, q_rs).wait()
        q_copy(k, do_ref, dog, do_ss, do_rs).wait()
    loc_q.wait()
    loc_do.wait()
    kv_sib_wait(jnp.int32(0))
    attn_first(z, True)
    kv_step(jnp.int32(5))

    def attn_step(s, _):
        kv_sib_wait(s)
        attn_first(z - s, False)

        @pl.when(s <= 2)
        def _():
            kv_step(s + 5)

        return 0

    near = jnp.minimum(z, 3)
    lax.fori_loop(1, near + 1, attn_step, 0)

    sin_f[...] = zero_s
    sin_b[...] = zero_s
    for k in range(NZ - 1, 0, -1):
        @pl.when(z - k >= 0)
        def _(k=k):
            rcopy(
                zmsg_up, zrecv_up.at[k], eu_ss.at[k], eu_rs.at[k], {"ctx": sib}
            ).wait_recv()
            rcopy(ztot, ztr_up.at[k], ut_ss.at[k], ut_rs.at[k], {"ctx": sib}).wait_recv()
            dec = jnp.exp2(rslice * get_total(ztr_up.at[k]))
            sin_f[...] = dec * sin_f[...] + zrecv_up[k].astype(F32)

        @pl.when(z + k < NZ)
        def _(k=k):
            rcopy(
                zmsg_dn, zrecv_dn.at[k], ed_ss.at[k], ed_rs.at[k], {"ctx": sib}
            ).wait_recv()
            rcopy(ztot, ztr_dn.at[k], dt_ss.at[k], dt_rs.at[k], {"ctx": sib}).wait_recv()
            dec = jnp.exp2(rslice * get_total(ztr_dn.at[k]))
            sin_b[...] = dec * sin_b[...] + zrecv_dn[k].astype(F32)
    for j in range(PLANE):
        cbuf[j, 0:NST, :] = (
            pre_f[j, 0:NST, :] + pre_f[j, NST:2 * NST, :] * sin_f[...]
        ).astype(BF16)
        cbuf[j, NST:2 * NST, :] = (
            pre_b[j, 0:NST, :] + pre_b[j, NST:2 * NST, :] * sin_b[...]
        ).astype(BF16)

    def c_copy(k):
        dst = plane_peer(k)
        return rcopy(cbuf.at[dst], crecv.at[p], ec_ss.at[k], ec_rs.at[k], {"ctx": base + dst})

    for k in range(1, PLANE):
        c_copy(k).start()
    crecv[p] = cbuf[p]

    lax.fori_loop(near + 1, z + 1, attn_step, 0)

    m8 = mst[...]
    m1 = jnp.max(m8, axis=0, keepdims=True)
    w8 = jnp.exp2(m8 - m1)
    l1 = jnp.sum(lst[...] * w8, axis=0, keepdims=True)
    r1 = jnp.sum(rst[...] * w8, axis=0, keepdims=True)
    n_rt = 2 * 1024 // 128
    for j in range(n_rt):
        cut = slice(j * 128, (j + 1) * 128)
        stat[0, j:j + 1, :] = m1[:, cut]
        stat[0, n_rt + j:n_rt + j + 1, :] = l1[:, cut]
        stat[0, 2 * n_rt + j:2 * n_rt + j + 1, :] = r1[:, cut]

    def stat_copy(k):
        dst = base + ((xx + k) % 4) * 2 + core
        return rcopy(stat.at[0], stat.at[k], sx_ss.at[k], sx_rs.at[k], {"ctx": dst})

    for k in range(1, 4):
        stat_copy(k).start()

    def second_chunk(ch, _):
        lanes = pl.ds(pl.multiple_of(ch * CW, CW), CW)
        rt = ratel[:, lanes]
        per = CW // slice_w
        h_in = jnp.concatenate([crecv[ch * per + i, 0:NST, :] for i in range(per)], axis=1).astype(F32)
        g_in = jnp.concatenate([crecv[ch * per + i, NST:2 * NST, :] for i in range(per)], axis=1).astype(F32)
        h_end = hs[TOK * NST:(TOK + 1) * NST, lanes] + jnp.exp2(
            rt * cum[TOK:TOK + 1, lanes]
        ) * h_in

        def folded(v):
            out = v[:, 0:128]
            for i in range(1, CW // 128):
                out = out + v[:, i * 128:(i + 1) * 128]
            return out

        def backward(i, both):
            carry, h_now = both
            lo = TOK // 8 - 1 - i
            for j in range(7, -1, -1):
                t = 8 * lo + j
                at = pl.ds(pl.multiple_of(t * NST, NST), NST)
                bt = jnp.tile(bb[at, :], (1, CW // 128))
                ct = jnp.tile(cb[at, :], (1, CW // 128))
                gyt = gyf[pl.ds(t, 1), lanes]
                gn = ct * gyt + carry
                carry = avs[at, lanes] * gn
                h_before = hs[at, lanes] + jnp.exp2(rt * cum[pl.ds(t, 1), lanes]) * h_in
                qv = carry * rt * h_before
                gb = gn * bt
                for v in range(CW // 128):
                    cut = slice(v * 128, (v + 1) * 128)
                    sg[v, j * 8:(j + 1) * 8, :] = gb[0:8, cut] + gb[8:16, cut]
                    sq[v, j * 8:(j + 1) * 8, :] = qv[0:8, cut] + qv[8:16, cut]
                wacc[at, :] += folded(gn * uf[pl.ds(t, 1), lanes])
                racc[at, :] += folded(h_now * gyt)
                h_now = h_before
            rows = pl.ds(pl.multiple_of(8 * lo, 8), 8)
            for v in range(CW // 128):
                cut = slice(v * 128, (v + 1) * 128)
                a1 = sg[v, pl.ds(0, 8, stride=8), :]
                a2 = sq[v, pl.ds(0, 8, stride=8), :]
                for n in range(1, 8):
                    a1 = a1 + sg[v, pl.ds(n, 8, stride=8), :]
                    a2 = a2 + sq[v, pl.ds(n, 8, stride=8), :]
                s1[rows, cut] = a1
                s2[rows, cut] = a2
            return carry, h_now

        lax.fori_loop(0, TOK // 8, backward, (g_in, h_end))
        gx_ref[:, lanes] = (s1[...] * stf[:, lanes]).astype(BF16)
        gs_ref[:, lanes] = (
            s1[...] * xb[:, lanes].astype(F32) + LN2 * s2[...]
        ).astype(BF16)
        return 0

    def y_copy(k):
        return rcopy(wred, yrecv.at[k], y_ss.at[k], y_rs.at[k], {"grp": gz + (y + k) % 4})

    h_copy = rcopy(hsum, hrecv, hh_ss, hh_rs, {"grp": (g + 4) % 8})

    def states_here():
        for k in range(1, PLANE):
            c_copy(k).wait()
        wacc[...] = jnp.zeros_like(wacc)
        racc[...] = jnp.zeros_like(racc)

    def coefficients():
        ones = jnp.ones((8, 256), BF16)
        for n in range(NST):
            for acc, to in ((wacc, n), (racc, NST + n)):
                part = acc[pl.ds(n, TOK, stride=NST), :]
                high = part.astype(BF16)
                low = (part - high.astype(F32)).astype(BF16)
                total = dot(ones, jnp.concatenate([high, low], axis=1), ((1,), (1,)))
                wred[to:to + 1, :] = total[0:1, :]

        for k in range(1, 4):
            y_copy(k).start()

    def across_z_hi():
        for k in range(1, 4):
            y_copy(k).wait()
        hsum[...] = wred[...] + yrecv[1] + yrecv[2] + yrecv[3]
        h_copy.start()

    def all_stats():
        for k in range(1, 4):
            stat_copy(k).wait()
        m4 = [stat[k, 0:n_rt, :] for k in range(4)]
        m_all = jnp.maximum(jnp.maximum(m4[0], m4[1]), jnp.maximum(m4[2], m4[3]))
        l_all = jnp.zeros((n_rt, 128), F32)
        r_all = jnp.zeros((n_rt, 128), F32)
        for k in range(4):
            w = jnp.exp2(m4[k] - m_all)
            l_all = l_all + w * stat[k, n_rt:2 * n_rt, :]
            r_all = r_all + w * stat[k, 2 * n_rt:3 * n_rt, :]
        lse_t = m_all + jnp.log2(l_all)
        rd_t = r_all / l_all
        for j in range(n_rt):
            cut = slice(j * 128, (j + 1) * 128)
            lse[:, cut] = jnp.broadcast_to(lse_t[j:j + 1, :], (8, 128))
            rdt[:, cut] = jnp.broadcast_to(rd_t[j:j + 1, :], (8, 128))

    dqt[...] = jnp.zeros_like(dqt)

    def attn_second(s, slot, diagonal):
        keys_t = kvg[slot, :, 0:HD].T

        def body(ch, carry):
            dk, dv = carry
            rows, cols, lanes = tile_of(ch)
            keys = kvg[slot, :, 0:HD]
            sc = dot(keys, qg[rows, cols], ((1,), (1,))) * (SCALE * LOG2E)
            pr = jnp.exp2(sc.reshape(2 * TOK // 8, 8, ROWS) - lse[:, lanes][None])
            if diagonal:
                pr = jnp.where(seen(ch).reshape(pr.shape), pr, 0.0)
            dp = dot(kvg[slot, :, HD:2 * HD], dog[rows, cols], ((1,), (1,)))
            ds = pr * (dp.reshape(pr.shape) - rdt[:, lanes][None])
            pb = pr.reshape(2 * TOK, ROWS).astype(BF16)
            db = ds.reshape(2 * TOK, ROWS).astype(BF16)
            dv = dv + dot(pb, dog[rows, cols], ((1,), (0,)))
            dk = dk + dot(db, qg[rows, cols], ((1,), (0,)))
            head = pl.ds(pl.multiple_of((ch // (1024 // ROWS)) * HD, HD), HD)
            dqt[head, rows] += dot(keys_t, db, ((1,), (0,)))
            return dk, dv

        zero = jnp.zeros((2 * TOK, HD), F32)
        dk, dv = lax.fori_loop(0, 2 * 1024 // ROWS, body, (zero, zero), unroll=True)
        dk = dk * SCALE
        first = core == 0
        own[s, :, 0:HD] = jnp.where(first, dk[0:TOK], dk[TOK:])
        own[s, :, HD:2 * HD] = jnp.where(first, dv[0:TOK], dv[TOK:])
        sib_s[s, :, 0:HD] = jnp.where(first, dk[TOK:], dk[0:TOK])
        sib_s[s, :, HD:2 * HD] = jnp.where(first, dv[TOK:], dv[0:TOK])
        sib_copy(s).start()

    def sib_copy(s):
        return rcopy(sib_s.at[s], sib_r.at[s], si_ss.at[s], si_rs.at[s], {"ctx": sib})

    def z_copy(s):
        return rcopy(
            zs.at[s], zr.at[s], zz_ss.at[s], zz_rs.at[s], {"ctx": c - s * PLANE}
        )

    def hand_down(s):
        sib_copy(s).wait()
        zs[s] = (own[s] + sib_r[s]).astype(BF16)
        z_copy(s).start()

    turn = jnp.maximum(z - 3, 0)

    def second_step(i, _):
        s = z - i

        @pl.when(i == 0)
        def _():
            states_here()

        @pl.when(jnp.logical_or(i == 0, i == turn))
        def _():
            first = jnp.where(i == 0, 0, 1)
            last = jnp.where(i == turn, n_chunks, 1)
            lax.fori_loop(first, last, second_chunk, 0)

        @pl.when(i == turn)
        def _():
            coefficients()

        @pl.when(i == 0)
        def _():
            all_stats()

        @pl.when(i < z)
        def _():
            attn_second(s, z - s, False)

        @pl.when(i == z)
        def _():
            attn_second(jnp.int32(0), z, True)

        @pl.when(i > 0)
        def _():
            hand_down(s + 1)

        @pl.when(i == jnp.minimum(turn + 2, z))
        def _():
            across_z_hi()

        return 0

    lax.fori_loop(0, z + 1, second_step, 0)

    dqs[...] = (dqt[...] * SCALE).astype(BF16)

    def dq_copy(k):
        dst = plane_peer(k)
        cols = pl.ds(pl.multiple_of(dst * TOK, TOK), TOK)
        return rcopy(
            dqs.at[:, cols], dqr.at[p], dq_ss.at[k], dq_rs.at[k], {"ctx": base + dst}
        )

    for k in range(1, PLANE):
        dq_copy(k).start()
    own_dq = pltpu.make_async_copy(
        dqs.at[:, pl.ds(pl.multiple_of(p * TOK, TOK), TOK)], dqr.at[p], loc.at[4]
    )
    own_dq.start()
    sib_copy(jnp.int32(0)).wait()

    for k in range(1, PLANE):
        dq_copy(k).wait()
    own_dq.wait()
    for cc in range(2):
        tot = dqr[cc].astype(F32)
        for i in range(1, 4):
            tot = tot + dqr[2 * i + cc].astype(F32)
        for h in range(2):
            col = (cc * 2 + h) * HD
            dq_ref[:, col:col + HD] = tot[h * HD:(h + 1) * HD, :].T.astype(BF16)

    own[0] = own[0] + sib_r[0]
    for k in range(1, NZ):
        @pl.when(z + k < NZ)
        def _(k=k):
            rcopy(zs.at[k], zr.at[k], zz_ss.at[k], zz_rs.at[k], {"ctx": sib}).wait_recv()
            own[0] = own[0] + zr[k].astype(F32)
    dk_ref[...] = own[0, :, 0:HD].astype(BF16)
    dv_ref[...] = own[0, :, HD:2 * HD].astype(BF16)

    h_copy.wait()
    gw_ref[...] = hsum[0:NST, :] + hrecv[0:NST, :]
    gr_ref[...] = hsum[NST:2 * NST, :] + hrecv[NST:2 * NST, :]

    for k in range(1, NZ):
        @pl.when(z + k < NZ)
        def _(k=k):
            up_copy(k).wait_send()
            upt_copy(k).wait_send()

        @pl.when(z - k >= 0)
        def _(k=k):
            dn_copy(k).wait_send()
            dnt_copy(k).wait_send()
            z_copy(k).wait_send()
    for s in range(NZ):
        @pl.when(z - s >= 0)
        def _(s=s):
            kv_over(s, z - s).wait_send()

            @pl.when(z < NZ - 1)
            def _():
                for piece in range(TOK // KV_ROWS):
                    kv_up(s, z - s, piece).wait_send()


def hand_over(*refs):
    copies = [pltpu.make_async_copy(refs[i], refs[7 + i], refs[14].at[i]) for i in range(7)]
    for copy in copies:
        copy.start()
    for copy in copies:
        copy.wait()


def on_device(
    queries, key_vectors, value_vectors, grad_attn, mamba_input, step_sizes, decay_rates,
    write_coef, read_coef, grad_mamba,
):
    channels = mamba_input.shape[1]
    slice_w = channels // PLANE
    vmem = pltpu.VMEM
    dma = pltpu.SemaphoreType.DMA
    scratch = [
        vmem((TOK, channels), BF16), vmem((TOK, channels), BF16), vmem((TOK, channels), BF16),
        vmem((NST, channels), F32), vmem((2 * NST, TOK), F32), vmem((128, 128), F32),
        vmem((1024, 256), BF16), vmem((1024, 256), BF16), vmem((NZ, 256, 256), BF16),
        vmem((TOK, channels), F32), vmem((TOK, channels), F32), vmem((TOK, channels), F32),
        vmem((TOK * NST, 128), F32), vmem((TOK * NST, 128), F32), vmem((128, 128), F32),
        vmem((NST, channels), F32),
        vmem((PLANE, 32, slice_w), BF16), vmem((PLANE, 32, slice_w), BF16),
        vmem((NST, slice_w), BF16), vmem((NST, slice_w), BF16),
        vmem((NZ, NST, slice_w), BF16), vmem((NZ, NST, slice_w), BF16),
        vmem((PLANE, 32, slice_w), F32), vmem((PLANE, 32, slice_w), F32),
        vmem((NST, slice_w), F32), vmem((NST, slice_w), F32),
        vmem((PLANE, 32, slice_w), BF16), vmem((PLANE, 32, slice_w), BF16),
        vmem((8, 2048), F32), vmem((8, 2048), F32), vmem((8, 2048), F32),
        vmem((4, 48, 128), F32), vmem((8, 2048), F32), vmem((8, 2048), F32),
        vmem((256, 1024), F32), vmem((256, 1024), BF16), vmem((PLANE, 256, 128), BF16),
        vmem((NZ, 128, 256), F32), vmem((NZ, 128, 256), F32), vmem((NZ, 128, 256), F32),
        vmem((NZ, 128, 256), BF16), vmem((NZ, 128, 256), BF16),
        vmem(((TOK + 1) * NST, channels), F32), vmem((TOK * NST, channels), F32),
        vmem((TOK + 8, channels), F32),
        vmem((CW // 128, 64, 128), F32), vmem((CW // 128, 64, 128), F32), vmem((TOK, CW), F32), vmem((TOK, CW), F32),
        vmem((TOK * NST, 128), F32), vmem((TOK * NST, 128), F32),
        vmem((32, 128), F32), vmem((4, 32, 128), F32), vmem((32, 128), F32), vmem((32, 128), F32),
        dma((8,)), dma((8,)), dma((8,)), dma((8,)),
        dma((8, TOK // KV_ROWS)), dma((8, TOK // KV_ROWS)), dma((8,)), dma((8,)),
        dma((8,)),
        dma((8,)), dma((8,)), dma((8,)), dma((8,)), dma((8,)), dma((8,)), dma((8,)), dma((8,)),
        dma((4,)), dma((4,)), dma((8,)), dma((8,)), dma((8,)), dma((8,)), dma((8,)), dma((8,)),
        dma((4,)), dma((4,)), dma, dma, dma((8,)),
        vmem((PLANE, slice_w // 128, 128), F32), vmem((PLANE, slice_w // 128, 128), F32),
        vmem((slice_w // 128, 128), F32),
        vmem((NZ, slice_w // 128, 128), F32), vmem((NZ, slice_w // 128, 128), F32),
        dma((8,)), dma((8,)), dma((8,)), dma((8,)), dma((8,)), dma((8,)),
    ]
    outs = (
        jax.ShapeDtypeStruct(queries.shape, BF16),
        jax.ShapeDtypeStruct(key_vectors.shape, BF16),
        jax.ShapeDtypeStruct(value_vectors.shape, BF16),
        jax.ShapeDtypeStruct(mamba_input.shape, BF16),
        jax.ShapeDtypeStruct(step_sizes.shape, BF16),
        jax.ShapeDtypeStruct((NST, TOK), F32),
        jax.ShapeDtypeStruct((NST, TOK), F32),
    )
    made = pl.pallas_call(
        kernel,
        out_shape=outs,
        in_specs=[pl.BlockSpec(memory_space=pl.ANY)] * 10,
        out_specs=(pl.BlockSpec(memory_space=pltpu.VMEM),) * 7,
        scratch_shapes=scratch,
        compiler_params=pltpu.CompilerParams(
            collective_id=0, has_side_effects=True, vmem_limit_bytes=60 * 2**20
        ),
    )(
        queries, key_vectors, value_vectors, grad_attn, mamba_input, step_sizes, decay_rates,
        write_coef.T, read_coef.T, grad_mamba,
    )
    out = pl.pallas_call(
        hand_over,
        out_shape=outs,
        in_specs=[pl.BlockSpec(memory_space=pltpu.VMEM)] * 7,
        out_specs=(pl.BlockSpec(memory_space=pltpu.HBM),) * 7,
        scratch_shapes=[dma((7,))],
    )(*made)
    return out[:5] + (out[5].T, out[6].T)


def solution(mesh):
    both = P("ctx", "grp")
    rows = P("ctx", None)
    return jax.shard_map(
        on_device,
        mesh=mesh,
        in_specs=(both,) * 6 + (P(None, "grp"), rows, rows, both),
        out_specs=(both,) * 5 + (rows, rows),
        check_vma=False,
    )
```

```python
import math

import jax
import jax.numpy as jnp
from jax import lax
from jax.experimental import pallas as pl
from jax.experimental.pallas import tpu as pltpu
from jax.sharding import PartitionSpec as P

MESH = pl.DeviceIdType.MESH
F32 = jnp.float32
BF16 = jnp.bfloat16
HD = 128
NST = 16
TOK = 128
PLANE = 8
NZ = 8
LOG2E = 1.4426950408889634
LN2 = 0.6931471805599453
SCALE = 1.0 / math.sqrt(HD)
NEG = -1e30
CW = 512
ROWS = 512
FAR = 4
KV_ROWS = 32


def dot(a, b, dims):
    return lax.dot_general(a, b, (dims, ((), ())), preferred_element_type=F32)


def kernel(
    q_ref, k_ref, v_ref, do_ref, x_ref, st_ref, rate_ref, b_ref, c_ref, gy_ref,
    dq_ref, dk_ref, dv_ref, gx_ref, gs_ref, gw_ref, gr_ref,
    gxb, gsb, xb, stb, gyb, rates, bct, spr, qg, dog, kvg, stf, uf, gyf, bb, cb, tmp, ratel,
    ebuf, erecv, zmsg_up, zmsg_dn, zrecv_up, zrecv_dn, pre_f, pre_b, sin_f, sin_b, cbuf, crecv,
    mst, lst, rst, stat, lse, rdt,
    dqt, dqs, dqr, own, sib_s, sib_r, zs, zr,
    hs, avs, cum, sg, sq, s1, s2, wacc, racc, wred, yrecv, hsum, hrecv,
    q_ss, q_rs, do_ss, do_rs, kz_ss, kz_rs, kf_ss, ks_ss, ks_rs, loc,
    ea_ss, ea_rs, eu_ss, eu_rs, ed_ss, ed_rs, ec_ss, ec_rs,
    sx_ss, sx_rs, dq_ss, dq_rs, si_ss, si_rs, zz_ss, zz_rs, y_ss, y_rs, hh_ss, hh_rs, ld,
    etot, ertot, ztot, ztr_up, ztr_dn, et_ss, et_rs, ut_ss, ut_rs, dt_ss, dt_rs,
):
    channels = xb.shape[1]
    n_chunks = channels // CW
    slice_w = channels // PLANE
    c = lax.axis_index("ctx")
    g = lax.axis_index("grp")
    z = c // PLANE
    p = c % PLANE
    xx = p // 2
    core = p % 2
    sib = c + 1 - 2 * core
    base = z * PLANE
    y = g % 4
    gz = g - y

    def plane_peer(k):
        return (p + k) % PLANE

    def plane_from(k):
        return (p + PLANE - k) % PLANE

    def rcopy(src, dst, ss, rs, dev):
        return pltpu.make_async_remote_copy(
            src_ref=src, dst_ref=dst, send_sem=ss, recv_sem=rs, device_id=dev, device_id_type=MESH
        )

    bar = pltpu.get_barrier_semaphore()

    def greet(dev):
        pl.semaphore_signal(bar, inc=1, device_id=dev, device_id_type=MESH)

    key_rows = pl.ds(pl.multiple_of(core * TOK, TOK), TOK)
    loads = [
        pltpu.make_async_copy(src, dst, ld.at[i])
        for i, (src, dst) in enumerate((
            (st_ref, stb), (x_ref, xb), (gy_ref, gyb), (rate_ref, rates),
            (b_ref, bct.at[0:NST, :]), (c_ref, bct.at[NST:2 * NST, :]),
            (k_ref, kvg.at[z, key_rows, 0:HD]), (v_ref, kvg.at[z, key_rows, HD:2 * HD]),
        ))
    ]
    loads[4].start()
    loads[5].start()
    greet({"grp": (g + 4) % 8})
    for k in (4, 3, 5, 2, 6, 1, 7):
        greet({"ctx": ((z + k) % NZ) * PLANE + p})
    for k in range(1, 4):
        greet({"grp": gz + (y + k) % 4})
    for k in range(1, PLANE):
        greet({"ctx": base + plane_peer(k)})
    for load in loads[0:4] + loads[6:8]:
        load.start()

    loads[4].wait()
    loads[5].wait()
    exact = bct[...]
    tmp[...] = jnp.zeros_like(tmp)
    for i in range(3):
        piece = exact.astype(BF16).astype(F32)
        tmp[2 * NST * i:2 * NST * (i + 1), :] = piece
        exact = exact - piece
    spr[...] = tmp[...].T
    own_state = (
        lax.broadcasted_iota(jnp.int32, (NST, 128), 1) % NST
        == lax.broadcasted_iota(jnp.int32, (NST, 128), 0)
    )
    pick = jnp.where(
        (lax.broadcasted_iota(jnp.int32, (128, 256), 0) // NST) % 2
        == lax.broadcasted_iota(jnp.int32, (128, 256), 1) // 128,
        1.0, 0.0,
    ).astype(BF16)

    def spread(i, _):
        rows = [
            jnp.where(own_state, jnp.broadcast_to(spr[pl.ds(8 * i + j, 1), :], (NST, 128)), 0.0)
            for j in range(8)
        ]
        both = dot(jnp.concatenate(rows, axis=0).astype(BF16), pick, ((1,), (0,)))
        at = pl.ds(pl.multiple_of(8 * i * NST, 8 * NST), 8 * NST)
        bb[at, :] = both[:, 0:128]
        cb[at, :] = both[:, 128:256]
        return 0

    lax.fori_loop(0, TOK // 8, spread, 0, unroll=4)
    for load in loads[0:4]:
        load.wait()
    stf[...] = stb[...].astype(F32)
    uf[...] = stf[...] * xb[...].astype(F32)
    gyf[...] = gyb[...].astype(F32)
    ratel[...] = rates[...] * (-LOG2E)
    def put_total(ref, row):
        for i in range(slice_w // 128):
            ref[i:i + 1, :] = row[:, i * 128:(i + 1) * 128]

    def get_total(ref):
        return jnp.concatenate([ref[i:i + 1, :] for i in range(slice_w // 128)], axis=1)

    earlier = jnp.where(
        lax.broadcasted_iota(jnp.int32, (TOK + 8, TOK), 0)
        > lax.broadcasted_iota(jnp.int32, (TOK + 8, TOK), 1),
        1.0, 0.0,
    ).astype(BF16)

    def first_chunk(ch, _):
        lanes = pl.ds(pl.multiple_of(ch * CW, CW), CW)
        rt = ratel[:, lanes]

        def body(i, carry):
            h, pr, gg = carry
            for j in range(8):
                t = 8 * i + j
                at = pl.ds(pl.multiple_of(t * NST, NST), NST)
                bt = jnp.tile(bb[at, :], (1, CW // 128))
                ct = jnp.tile(cb[at, :], (1, CW // 128))
                a = jnp.exp2(rt * stf[pl.ds(t, 1), lanes])
                avs[at, lanes] = a
                h = a * h + uf[pl.ds(t, 1), lanes] * bt
                hs[pl.ds(pl.multiple_of((t + 1) * NST, NST), NST), lanes] = h
                pr = a * pr
                gg = gg + pr * (gyf[pl.ds(t, 1), lanes] * ct)
            return (h, pr, gg)

        zero = jnp.zeros((NST, CW), F32)
        hs[0:NST, lanes] = zero
        h, pr, gg = lax.fori_loop(0, TOK // 8, body, (zero, jnp.ones((NST, CW), F32), zero))
        before = dot(earlier, stb[:, lanes], ((1,), (0,)))
        total = before[TOK:TOK + 1, :]
        cum[:, lanes] = before
        for half in range(CW // slice_w):
            to = ch * (CW // slice_w) + half
            cut = slice(half * slice_w, (half + 1) * slice_w)
            ebuf[to, 0:NST, :] = h[:, cut].astype(BF16)
            ebuf[to, NST:2 * NST, :] = gg[:, cut].astype(BF16)
            put_total(etot.at[to], total[:, cut])
        return 0

    lax.fori_loop(0, 1, first_chunk, 0)
    loads[6].wait()
    loads[7].wait()

    pl.semaphore_wait(bar, PLANE - 1 + NZ - 1 + 3 + 1)

    def q_copy(k, whole, gathered, ss, rs):
        dst = plane_peer(k)
        cols = pl.ds(pl.multiple_of((dst % 2) * 2 * HD, 2 * HD), 2 * HD)
        rows = pl.ds(pl.multiple_of(p * TOK, TOK), TOK)
        return rcopy(
            whole.at[:, cols], gathered.at[rows, :], ss.at[k], rs.at[k], {"ctx": base + dst}
        )

    def kv_part(slot, piece):
        at = core * TOK + piece * KV_ROWS
        return kvg.at[slot, pl.ds(pl.multiple_of(at, KV_ROWS), KV_ROWS), :]

    def kv_up(s, slot, piece):
        part = kv_part(slot, piece)
        return rcopy(part, part, kz_ss.at[s, piece], kz_rs.at[s + 1, piece], {"ctx": c + PLANE})

    def kv_far(piece):
        part = kv_part(z, piece)
        return rcopy(
            part, part, kf_ss.at[piece], kz_rs.at[FAR, piece], {"ctx": c + FAR * PLANE}
        )

    def kv_over(s, slot):
        part = kvg.at[slot, pl.ds(pl.multiple_of(core * TOK, TOK), TOK), :]
        return rcopy(part, part, ks_ss.at[s], ks_rs.at[s], {"ctx": sib})

    def kv_step(s):
        slot = z - s

        @pl.when(slot >= 0)
        def _():
            for piece in range(TOK // KV_ROWS):
                @pl.when(s > 0)
                def _():
                    part = kv_part(slot, piece)
                    rcopy(
                        part, part, kz_ss.at[s, piece], kz_rs.at[s, piece], {"ctx": sib}
                    ).wait_recv()

                @pl.when(jnp.logical_and(z < NZ - 1, s != FAR - 1))
                def _():
                    kv_up(s, slot, piece).start()

            kv_over(s, slot).start()

    def kv_sib_wait(s):
        part = kvg.at[z - s, pl.ds(pl.multiple_of((1 - core) * TOK, TOK), TOK), :]
        rcopy(part, part, ks_ss.at[s], ks_rs.at[s], {"ctx": sib}).wait_recv()

    kv_step(jnp.int32(0))

    for k in range(1, PLANE):
        q_copy(k, q_ref, qg, q_ss, q_rs).start()
    my_cols = pl.ds(pl.multiple_of(core * 2 * HD, 2 * HD), 2 * HD)
    my_rows = pl.ds(pl.multiple_of(p * TOK, TOK), TOK)
    loc_q = pltpu.make_async_copy(q_ref.at[:, my_cols], qg.at[my_rows, :], loc.at[0])
    loc_do = pltpu.make_async_copy(do_ref.at[:, my_cols], dog.at[my_rows, :], loc.at[1])
    loc_q.start()
    loc_do.start()

    def first_step(ch, _):
        first_chunk(ch, 0)

        @pl.when(jnp.logical_and(ch == 1, z < NZ - FAR))
        def _():
            for piece in range(TOK // KV_ROWS):
                kv_far(piece).start()

        @pl.when(ch == 2)
        def _():
            kv_step(jnp.int32(1))

        return 0

    lax.fori_loop(1, n_chunks, first_step, 0)

    def e_copy(k):
        dst = plane_peer(k)
        return rcopy(ebuf.at[dst], erecv.at[p], ea_ss.at[k], ea_rs.at[k], {"ctx": base + dst})

    def et_copy(k):
        dst = plane_peer(k)
        return rcopy(etot.at[dst], ertot.at[p], et_ss.at[k], et_rs.at[k], {"ctx": base + dst})

    for k in range(1, PLANE):
        e_copy(k).start()
        et_copy(k).start()
    for k in range(1, PLANE):
        q_copy(k, do_ref, dog, do_ss, do_rs).start()
    erecv[p] = ebuf[p]
    ertot[p] = etot[p]

    mst[...] = jnp.full(mst.shape, NEG, F32)
    lst[...] = jnp.zeros_like(lst)
    rst[...] = jnp.zeros_like(rst)

    def tile_of(ch):
        head = ch // (1024 // ROWS)
        rows = pl.ds(pl.multiple_of((ch % (1024 // ROWS)) * ROWS, ROWS), ROWS)
        cols = pl.ds(pl.multiple_of(head * HD, HD), HD)
        lanes = pl.ds(pl.multiple_of(ch * ROWS, ROWS), ROWS)
        return rows, cols, lanes

    def seen(ch):
        key = xx * 2 * TOK + lax.broadcasted_iota(jnp.int32, (2 * TOK, ROWS), 0)
        query = (ch % (1024 // ROWS)) * ROWS + lax.broadcasted_iota(jnp.int32, (2 * TOK, ROWS), 1)
        return key <= query

    def attn_first(slot, diagonal):
        def body(ch, _):
            rows, cols, lanes = tile_of(ch)
            sc = dot(kvg[slot, :, 0:HD], qg[rows, cols], ((1,), (1,))) * (SCALE * LOG2E)
            if diagonal:
                sc = jnp.where(seen(ch), sc, NEG)
            sc = sc.reshape(2 * TOK // 8, 8, ROWS)
            dp = dot(kvg[slot, :, HD:2 * HD], dog[rows, cols], ((1,), (1,)))
            dp = dp.reshape(2 * TOK // 8, 8, ROWS)
            m_old = mst[:, lanes]
            m_new = jnp.maximum(m_old, jnp.max(sc, axis=0))
            shrink = jnp.exp2(m_old - m_new)
            pr = jnp.exp2(sc - m_new[None])
            mst[:, lanes] = m_new
            lst[:, lanes] = lst[:, lanes] * shrink + jnp.sum(pr, axis=0)
            rst[:, lanes] = rst[:, lanes] * shrink + jnp.sum(pr * dp, axis=0)
            return 0

        lax.fori_loop(0, 2 * 1024 // ROWS, body, 0, unroll=True)

    kv_step(jnp.int32(2))
    kv_step(jnp.int32(4))
    kv_step(jnp.int32(3))

    for k in range(1, PLANE):
        e_copy(k).wait()
        et_copy(k).wait()
    kv_step(jnp.int32(5))
    mine = pl.ds(pl.multiple_of(p * slice_w, slice_w), slice_w)
    rslice = ratel[:, mine]
    zero_s = jnp.zeros((NST, slice_w), F32)
    state = zero_s
    total = jnp.zeros((1, slice_w), F32)
    for j in range(PLANE):
        pre_f[j, 0:NST, :] = state
        pre_f[j, NST:2 * NST, :] = jnp.exp2(rslice * total)
        tj = get_total(ertot.at[j])
        state = jnp.exp2(rslice * tj) * state + erecv[j, 0:NST, :].astype(F32)
        total = total + tj
    plane_total = total
    zmsg_up[...] = state.astype(BF16)
    put_total(ztot, plane_total)
    state = zero_s
    total = jnp.zeros((1, slice_w), F32)
    for j in range(PLANE - 1, -1, -1):
        pre_b[j, 0:NST, :] = state
        pre_b[j, NST:2 * NST, :] = jnp.exp2(rslice * total)
        tj = get_total(ertot.at[j])
        state = jnp.exp2(rslice * tj) * state + erecv[j, NST:2 * NST, :].astype(F32)
        total = total + tj
    zmsg_dn[...] = state.astype(BF16)

    def up_copy(k):
        return rcopy(
            zmsg_up, zrecv_up.at[k], eu_ss.at[k], eu_rs.at[k], {"ctx": c + k * PLANE}
        )

    def dn_copy(k):
        return rcopy(
            zmsg_dn, zrecv_dn.at[k], ed_ss.at[k], ed_rs.at[k], {"ctx": c - k * PLANE}
        )

    def upt_copy(k):
        return rcopy(ztot, ztr_up.at[k], ut_ss.at[k], ut_rs.at[k], {"ctx": c + k * PLANE})

    def dnt_copy(k):
        return rcopy(ztot, ztr_dn.at[k], dt_ss.at[k], dt_rs.at[k], {"ctx": c - k * PLANE})

    for k in range(1, NZ):
        @pl.when(z + k < NZ)
        def _(k=k):
            upt_copy(k).start()
            up_copy(k).start()

        @pl.when(z - k >= 0)
        def _(k=k):
            dnt_copy(k).start()
            dn_copy(k).start()

    for k in range(1, PLANE):
        q_copy(k, q_ref, qg, q_ss, q_rs).wait()
        q_copy(k, do_ref, dog, do_ss, do_rs).wait()
    loc_q.wait()
    loc_do.wait()
    kv_sib_wait(jnp.int32(0))
    attn_first(z, True)
    kv_step(jnp.int32(6))

    def attn_step(s, _):
        kv_sib_wait(s)
        attn_first(z - s, False)

        @pl.when(s == 5)
        def _():
            kv_step(jnp.int32(7))

        return 0

    near = jnp.minimum(z, 3)
    lax.fori_loop(1, near + 1, attn_step, 0)

    sin_f[...] = zero_s
    sin_b[...] = zero_s
    for k in range(NZ - 1, 0, -1):
        @pl.when(z - k >= 0)
        def _(k=k):
            rcopy(
                zmsg_up, zrecv_up.at[k], eu_ss.at[k], eu_rs.at[k], {"ctx": sib}
            ).wait_recv()
            rcopy(ztot, ztr_up.at[k], ut_ss.at[k], ut_rs.at[k], {"ctx": sib}).wait_recv()
            dec = jnp.exp2(rslice * get_total(ztr_up.at[k]))
            sin_f[...] = dec * sin_f[...] + zrecv_up[k].astype(F32)

        @pl.when(z + k < NZ)
        def _(k=k):
            rcopy(
                zmsg_dn, zrecv_dn.at[k], ed_ss.at[k], ed_rs.at[k], {"ctx": sib}
            ).wait_recv()
            rcopy(ztot, ztr_dn.at[k], dt_ss.at[k], dt_rs.at[k], {"ctx": sib}).wait_recv()
            dec = jnp.exp2(rslice * get_total(ztr_dn.at[k]))
            sin_b[...] = dec * sin_b[...] + zrecv_dn[k].astype(F32)
    for j in range(PLANE):
        cbuf[j, 0:NST, :] = (
            pre_f[j, 0:NST, :] + pre_f[j, NST:2 * NST, :] * sin_f[...]
        ).astype(BF16)
        cbuf[j, NST:2 * NST, :] = (
            pre_b[j, 0:NST, :] + pre_b[j, NST:2 * NST, :] * sin_b[...]
        ).astype(BF16)

    def c_copy(k):
        dst = plane_peer(k)
        return rcopy(cbuf.at[dst], crecv.at[p], ec_ss.at[k], ec_rs.at[k], {"ctx": base + dst})

    for k in range(1, PLANE):
        c_copy(k).start()
    crecv[p] = cbuf[p]

    lax.fori_loop(near + 1, z + 1, attn_step, 0)

    m8 = mst[...]
    m1 = jnp.max(m8, axis=0, keepdims=True)
    w8 = jnp.exp2(m8 - m1)
    l1 = jnp.sum(lst[...] * w8, axis=0, keepdims=True)
    r1 = jnp.sum(rst[...] * w8, axis=0, keepdims=True)
    n_rt = 2 * 1024 // 128
    for j in range(n_rt):
        cut = slice(j * 128, (j + 1) * 128)
        stat[0, j:j + 1, :] = m1[:, cut]
        stat[0, n_rt + j:n_rt + j + 1, :] = l1[:, cut]
        stat[0, 2 * n_rt + j:2 * n_rt + j + 1, :] = r1[:, cut]

    def stat_copy(k):
        dst = base + ((xx + k) % 4) * 2 + core
        return rcopy(stat.at[0], stat.at[k], sx_ss.at[k], sx_rs.at[k], {"ctx": dst})

    for k in range(1, 4):
        stat_copy(k).start()

    def second_chunk(ch, _):
        lanes = pl.ds(pl.multiple_of(ch * CW, CW), CW)
        rt = ratel[:, lanes]
        per = CW // slice_w
        h_in = jnp.concatenate([crecv[ch * per + i, 0:NST, :] for i in range(per)], axis=1).astype(F32)
        g_in = jnp.concatenate([crecv[ch * per + i, NST:2 * NST, :] for i in range(per)], axis=1).astype(F32)
        h_end = hs[TOK * NST:(TOK + 1) * NST, lanes] + jnp.exp2(
            rt * cum[TOK:TOK + 1, lanes]
        ) * h_in

        def folded(v):
            out = v[:, 0:128]
            for i in range(1, CW // 128):
                out = out + v[:, i * 128:(i + 1) * 128]
            return out

        def backward(i, both):
            carry, h_now = both
            lo = TOK // 8 - 1 - i
            for j in range(7, -1, -1):
                t = 8 * lo + j
                at = pl.ds(pl.multiple_of(t * NST, NST), NST)
                bt = jnp.tile(bb[at, :], (1, CW // 128))
                ct = jnp.tile(cb[at, :], (1, CW // 128))
                gyt = gyf[pl.ds(t, 1), lanes]
                gn = ct * gyt + carry
                carry = avs[at, lanes] * gn
                h_before = hs[at, lanes] + jnp.exp2(rt * cum[pl.ds(t, 1), lanes]) * h_in
                qv = carry * rt * h_before
                gb = gn * bt
                for v in range(CW // 128):
                    cut = slice(v * 128, (v + 1) * 128)
                    sg[v, j * 8:(j + 1) * 8, :] = gb[0:8, cut] + gb[8:16, cut]
                    sq[v, j * 8:(j + 1) * 8, :] = qv[0:8, cut] + qv[8:16, cut]
                wacc[at, :] += folded(gn * uf[pl.ds(t, 1), lanes])
                racc[at, :] += folded(h_now * gyt)
                h_now = h_before
            rows = pl.ds(pl.multiple_of(8 * lo, 8), 8)
            for v in range(CW // 128):
                cut = slice(v * 128, (v + 1) * 128)
                a1 = sg[v, pl.ds(0, 8, stride=8), :]
                a2 = sq[v, pl.ds(0, 8, stride=8), :]
                for n in range(1, 8):
                    a1 = a1 + sg[v, pl.ds(n, 8, stride=8), :]
                    a2 = a2 + sq[v, pl.ds(n, 8, stride=8), :]
                s1[rows, cut] = a1
                s2[rows, cut] = a2
            return carry, h_now

        lax.fori_loop(0, TOK // 8, backward, (g_in, h_end))
        gxb[:, lanes] = (s1[...] * stf[:, lanes]).astype(BF16)
        gsb[:, lanes] = (
            s1[...] * xb[:, lanes].astype(F32) + LN2 * s2[...]
        ).astype(BF16)
        return 0

    def y_copy(k):
        return rcopy(wred, yrecv.at[k], y_ss.at[k], y_rs.at[k], {"grp": gz + (y + k) % 4})

    h_copy = rcopy(hsum, hrecv, hh_ss, hh_rs, {"grp": (g + 4) % 8})

    def states_here():
        for k in range(1, PLANE):
            c_copy(k).wait()
        wacc[...] = jnp.zeros_like(wacc)
        racc[...] = jnp.zeros_like(racc)

    gx_out = pltpu.make_async_copy(gxb, gx_ref, loc.at[5])
    gs_out = pltpu.make_async_copy(gsb, gs_ref, loc.at[6])

    def coefficients():
        gx_out.start()
        gs_out.start()
        ones = jnp.ones((8, 256), BF16)
        for n in range(NST):
            for acc, to in ((wacc, n), (racc, NST + n)):
                part = acc[pl.ds(n, TOK, stride=NST), :]
                high = part.astype(BF16)
                low = (part - high.astype(F32)).astype(BF16)
                total = dot(ones, jnp.concatenate([high, low], axis=1), ((1,), (1,)))
                wred[to:to + 1, :] = total[0:1, :]

        for k in range(1, 4):
            y_copy(k).start()

    def across_z_hi():
        for k in range(1, 4):
            y_copy(k).wait()
        hsum[...] = wred[...] + yrecv[1] + yrecv[2] + yrecv[3]
        h_copy.start()

    def all_stats():
        for k in range(1, 4):
            stat_copy(k).wait()
        m4 = [stat[k, 0:n_rt, :] for k in range(4)]
        m_all = jnp.maximum(jnp.maximum(m4[0], m4[1]), jnp.maximum(m4[2], m4[3]))
        l_all = jnp.zeros((n_rt, 128), F32)
        r_all = jnp.zeros((n_rt, 128), F32)
        for k in range(4):
            w = jnp.exp2(m4[k] - m_all)
            l_all = l_all + w * stat[k, n_rt:2 * n_rt, :]
            r_all = r_all + w * stat[k, 2 * n_rt:3 * n_rt, :]
        lse_t = m_all + jnp.log2(l_all)
        rd_t = r_all / l_all
        for j in range(n_rt):
            cut = slice(j * 128, (j + 1) * 128)
            lse[:, cut] = jnp.broadcast_to(lse_t[j:j + 1, :], (8, 128))
            rdt[:, cut] = jnp.broadcast_to(rd_t[j:j + 1, :], (8, 128))

    dqt[...] = jnp.zeros_like(dqt)

    def attn_second(s, slot, diagonal):
        keys_t = kvg[slot, :, 0:HD].T

        def body(ch, carry):
            dk, dv = carry
            rows, cols, lanes = tile_of(ch)
            keys = kvg[slot, :, 0:HD]
            sc = dot(keys, qg[rows, cols], ((1,), (1,))) * (SCALE * LOG2E)
            pr = jnp.exp2(sc.reshape(2 * TOK // 8, 8, ROWS) - lse[:, lanes][None])
            if diagonal:
                pr = jnp.where(seen(ch).reshape(pr.shape), pr, 0.0)
            dp = dot(kvg[slot, :, HD:2 * HD], dog[rows, cols], ((1,), (1,)))
            ds = pr * (dp.reshape(pr.shape) - rdt[:, lanes][None])
            pb = pr.reshape(2 * TOK, ROWS).astype(BF16)
            db = ds.reshape(2 * TOK, ROWS).astype(BF16)
            dv = dv + dot(pb, dog[rows, cols], ((1,), (0,)))
            dk = dk + dot(db, qg[rows, cols], ((1,), (0,)))
            head = pl.ds(pl.multiple_of((ch // (1024 // ROWS)) * HD, HD), HD)
            dqt[head, rows] += dot(keys_t, db, ((1,), (0,)))
            return dk, dv

        zero = jnp.zeros((2 * TOK, HD), F32)
        dk, dv = lax.fori_loop(0, 2 * 1024 // ROWS, body, (zero, zero), unroll=True)
        dk = dk * SCALE
        first = core == 0
        own[s, :, 0:HD] = jnp.where(first, dk[0:TOK], dk[TOK:])
        own[s, :, HD:2 * HD] = jnp.where(first, dv[0:TOK], dv[TOK:])
        sib_s[s, :, 0:HD] = jnp.where(first, dk[TOK:], dk[0:TOK])
        sib_s[s, :, HD:2 * HD] = jnp.where(first, dv[TOK:], dv[0:TOK])
        sib_copy(s).start()

    def sib_copy(s):
        return rcopy(sib_s.at[s], sib_r.at[s], si_ss.at[s], si_rs.at[s], {"ctx": sib})

    def z_copy(s):
        return rcopy(
            zs.at[s], zr.at[s], zz_ss.at[s], zz_rs.at[s], {"ctx": c - s * PLANE}
        )

    def hand_down(s):
        sib_copy(s).wait()
        zs[s] = (own[s] + sib_r[s]).astype(BF16)
        z_copy(s).start()

    turn = jnp.maximum(z - 2, 0)

    def second_step(i, _):
        s = z - i

        @pl.when(i == 0)
        def _():
            states_here()

        @pl.when(jnp.logical_or(i == 0, i == turn))
        def _():
            first = jnp.where(i == 0, 0, 1)
            last = jnp.where(i == turn, n_chunks, 1)
            lax.fori_loop(first, last, second_chunk, 0)

        @pl.when(i == turn)
        def _():
            coefficients()

        @pl.when(i == 0)
        def _():
            all_stats()

        @pl.when(i < z)
        def _():
            attn_second(s, z - s, False)

        @pl.when(i == z)
        def _():
            attn_second(jnp.int32(0), z, True)

        @pl.when(i > 0)
        def _():
            hand_down(s + 1)

        @pl.when(i == jnp.minimum(turn + 2, z))
        def _():
            across_z_hi()

        return 0

    lax.fori_loop(0, z + 1, second_step, 0)

    dqs[...] = (dqt[...] * SCALE).astype(BF16)

    def dq_copy(k):
        dst = plane_peer(k)
        cols = pl.ds(pl.multiple_of(dst * TOK, TOK), TOK)
        return rcopy(
            dqs.at[:, cols], dqr.at[p], dq_ss.at[k], dq_rs.at[k], {"ctx": base + dst}
        )

    for k in range(1, PLANE):
        dq_copy(k).start()
    own_dq = pltpu.make_async_copy(
        dqs.at[:, pl.ds(pl.multiple_of(p * TOK, TOK), TOK)], dqr.at[p], loc.at[4]
    )
    own_dq.start()
    sib_copy(jnp.int32(0)).wait()

    for k in range(1, PLANE):
        dq_copy(k).wait()
    own_dq.wait()
    for cc in range(2):
        tot = dqr[cc].astype(F32)
        for i in range(1, 4):
            tot = tot + dqr[2 * i + cc].astype(F32)
        for h in range(2):
            col = (cc * 2 + h) * HD
            dq_ref[:, col:col + HD] = tot[h * HD:(h + 1) * HD, :].T.astype(BF16)

    own[0] = own[0] + sib_r[0]
    for k in range(1, NZ):
        @pl.when(z + k < NZ)
        def _(k=k):
            rcopy(zs.at[k], zr.at[k], zz_ss.at[k], zz_rs.at[k], {"ctx": sib}).wait_recv()
            own[0] = own[0] + zr[k].astype(F32)
    dk_ref[...] = own[0, :, 0:HD].astype(BF16)
    dv_ref[...] = own[0, :, HD:2 * HD].astype(BF16)

    gx_out.wait()
    gs_out.wait()
    h_copy.wait()
    gw_ref[...] = hsum[0:NST, :] + hrecv[0:NST, :]
    gr_ref[...] = hsum[NST:2 * NST, :] + hrecv[NST:2 * NST, :]

    for k in range(1, NZ):
        @pl.when(z + k < NZ)
        def _(k=k):
            up_copy(k).wait_send()
            upt_copy(k).wait_send()

        @pl.when(z - k >= 0)
        def _(k=k):
            dn_copy(k).wait_send()
            dnt_copy(k).wait_send()
            z_copy(k).wait_send()
    for s in range(NZ):
        @pl.when(z - s >= 0)
        def _(s=s):
            kv_over(s, z - s).wait_send()

            if s != FAR - 1:
                @pl.when(z < NZ - 1)
                def _():
                    for piece in range(TOK // KV_ROWS):
                        kv_up(s, z - s, piece).wait_send()

    @pl.when(z < NZ - FAR)
    def _():
        for piece in range(TOK // KV_ROWS):
            kv_far(piece).wait_send()


def hand_over(*refs):
    copies = [pltpu.make_async_copy(refs[i], refs[7 + i], refs[14].at[i]) for i in range(7)]
    for copy in copies:
        copy.start()
    for copy in copies:
        copy.wait()


def on_device(
    queries, key_vectors, value_vectors, grad_attn, mamba_input, step_sizes, decay_rates,
    write_coef, read_coef, grad_mamba,
):
    channels = mamba_input.shape[1]
    slice_w = channels // PLANE
    vmem = pltpu.VMEM
    dma = pltpu.SemaphoreType.DMA
    scratch = [
        vmem((TOK, channels), BF16), vmem((TOK, channels), BF16),
        vmem((TOK, channels), BF16), vmem((TOK, channels), BF16), vmem((TOK, channels), BF16),
        vmem((NST, channels), F32), vmem((2 * NST, TOK), F32), vmem((128, 128), F32),
        vmem((1024, 256), BF16), vmem((1024, 256), BF16), vmem((NZ, 256, 256), BF16),
        vmem((TOK, channels), F32), vmem((TOK, channels), F32), vmem((TOK, channels), F32),
        vmem((TOK * NST, 128), F32), vmem((TOK * NST, 128), F32), vmem((128, 128), F32),
        vmem((NST, channels), F32),
        vmem((PLANE, 32, slice_w), BF16), vmem((PLANE, 32, slice_w), BF16),
        vmem((NST, slice_w), BF16), vmem((NST, slice_w), BF16),
        vmem((NZ, NST, slice_w), BF16), vmem((NZ, NST, slice_w), BF16),
        vmem((PLANE, 32, slice_w), F32), vmem((PLANE, 32, slice_w), F32),
        vmem((NST, slice_w), F32), vmem((NST, slice_w), F32),
        vmem((PLANE, 32, slice_w), BF16), vmem((PLANE, 32, slice_w), BF16),
        vmem((8, 2048), F32), vmem((8, 2048), F32), vmem((8, 2048), F32),
        vmem((4, 48, 128), F32), vmem((8, 2048), F32), vmem((8, 2048), F32),
        vmem((256, 1024), F32), vmem((256, 1024), BF16), vmem((PLANE, 256, 128), BF16),
        vmem((NZ, 128, 256), F32), vmem((NZ, 128, 256), F32), vmem((NZ, 128, 256), F32),
        vmem((NZ, 128, 256), BF16), vmem((NZ, 128, 256), BF16),
        vmem(((TOK + 1) * NST, channels), F32), vmem((TOK * NST, channels), F32),
        vmem((TOK + 8, channels), F32),
        vmem((CW // 128, 64, 128), F32), vmem((CW // 128, 64, 128), F32), vmem((TOK, CW), F32), vmem((TOK, CW), F32),
        vmem((TOK * NST, 128), F32), vmem((TOK * NST, 128), F32),
        vmem((32, 128), F32), vmem((4, 32, 128), F32), vmem((32, 128), F32), vmem((32, 128), F32),
        dma((8,)), dma((8,)), dma((8,)), dma((8,)),
        dma((8, TOK // KV_ROWS)), dma((8, TOK // KV_ROWS)), dma((TOK // KV_ROWS,)),
        dma((8,)), dma((8,)),
        dma((8,)),
        dma((8,)), dma((8,)), dma((8,)), dma((8,)), dma((8,)), dma((8,)), dma((8,)), dma((8,)),
        dma((4,)), dma((4,)), dma((8,)), dma((8,)), dma((8,)), dma((8,)), dma((8,)), dma((8,)),
        dma((4,)), dma((4,)), dma, dma, dma((8,)),
        vmem((PLANE, slice_w // 128, 128), F32), vmem((PLANE, slice_w // 128, 128), F32),
        vmem((slice_w // 128, 128), F32),
        vmem((NZ, slice_w // 128, 128), F32), vmem((NZ, slice_w // 128, 128), F32),
        dma((8,)), dma((8,)), dma((8,)), dma((8,)), dma((8,)), dma((8,)),
    ]
    outs = (
        jax.ShapeDtypeStruct(queries.shape, BF16),
        jax.ShapeDtypeStruct(key_vectors.shape, BF16),
        jax.ShapeDtypeStruct(value_vectors.shape, BF16),
        jax.ShapeDtypeStruct(mamba_input.shape, BF16),
        jax.ShapeDtypeStruct(step_sizes.shape, BF16),
        jax.ShapeDtypeStruct((NST, TOK), F32),
        jax.ShapeDtypeStruct((NST, TOK), F32),
    )
    made = pl.pallas_call(
        kernel,
        out_shape=outs,
        in_specs=[pl.BlockSpec(memory_space=pl.ANY)] * 10,
        out_specs=(pl.BlockSpec(memory_space=pltpu.VMEM),) * 3
        + (pl.BlockSpec(memory_space=pl.ANY),) * 2
        + (pl.BlockSpec(memory_space=pltpu.VMEM),) * 2,
        scratch_shapes=scratch,
        compiler_params=pltpu.CompilerParams(
            collective_id=0, has_side_effects=True, vmem_limit_bytes=60 * 2**20
        ),
    )(
        queries, key_vectors, value_vectors, grad_attn, mamba_input, step_sizes, decay_rates,
        write_coef.T, read_coef.T, grad_mamba,
    )
    out = pl.pallas_call(
        hand_over,
        out_shape=outs,
        in_specs=[pl.BlockSpec(memory_space=pltpu.VMEM)] * 7,
        out_specs=(pl.BlockSpec(memory_space=pltpu.HBM),) * 7,
        scratch_shapes=[dma((7,))],
    )(*made)
    return out[:5] + (out[5].T, out[6].T)


def solution(mesh):
    both = P("ctx", "grp")
    rows = P("ctx", None)
    return jax.shard_map(
        on_device,
        mesh=mesh,
        in_specs=(both,) * 6 + (P(None, "grp"), rows, rows, both),
        out_specs=(both,) * 5 + (rows, rows),
        check_vma=False,
    )
```

```python
import math

import jax
import jax.numpy as jnp
from jax import lax
from jax.experimental import pallas as pl
from jax.experimental.pallas import tpu as pltpu
from jax.sharding import PartitionSpec as P

MESH = pl.DeviceIdType.MESH
F32 = jnp.float32
BF16 = jnp.bfloat16
HD = 128
NST = 16
TOK = 128
PLANE = 8
NZ = 8
LOG2E = 1.4426950408889634
LN2 = 0.6931471805599453
SCALE = 1.0 / math.sqrt(HD)
NEG = -1e30
CW = 512
ROWS = 512
FIRST_FAR = (4, 3, 5, 2, 6, 1, 7)
FAR = 4
KV_ROWS = 32


def dot(a, b, dims):
    return lax.dot_general(a, b, (dims, ((), ())), preferred_element_type=F32)


def kernel(
    q_ref, k_ref, v_ref, do_ref, x_ref, st_ref, rate_ref, b_ref, c_ref, gy_ref,
    dq_ref, dk_ref, dv_ref, gx_ref, gs_ref, gw_ref, gr_ref,
    gxb, gsb, xb, stb, gyb, rates, bct, spr, qg, dog, kvg, stf, uf, gyf, bb, cb, tmp, ratel,
    ebuf, erecv, zmsg_up, zmsg_dn, zrecv_up, zrecv_dn, pre_f, pre_b, sin_f, sin_b, cbuf, crecv,
    mst, lst, rst, stat, lse, rdt,
    dqt, dqs, dqr, own, sib_s, sib_r, zs, zr,
    hs, avs, cum, sg, sq, s1, s2, wacc, racc, wred, yrecv, hsum, hrecv,
    q_ss, q_rs, do_ss, do_rs, kz_ss, kz_rs, kf_ss, ks_ss, ks_rs, loc,
    ea_ss, ea_rs, eu_ss, eu_rs, ed_ss, ed_rs, ec_ss, ec_rs,
    sx_ss, sx_rs, dq_ss, dq_rs, si_ss, si_rs, zz_ss, zz_rs, y_ss, y_rs, hh_ss, hh_rs, ld,
    etot, ertot, ztot, ztr_up, ztr_dn, et_ss, et_rs, ut_ss, ut_rs, dt_ss, dt_rs,
):
    channels = xb.shape[1]
    n_chunks = channels // CW
    slice_w = channels // PLANE
    c = lax.axis_index("ctx")
    g = lax.axis_index("grp")
    z = c // PLANE
    p = c % PLANE
    xx = p // 2
    core = p % 2
    sib = c + 1 - 2 * core
    base = z * PLANE
    y = g % 4
    gz = g - y

    def plane_peer(k):
        return (p + k) % PLANE

    def plane_from(k):
        return (p + PLANE - k) % PLANE

    def rcopy(src, dst, ss, rs, dev):
        return pltpu.make_async_remote_copy(
            src_ref=src, dst_ref=dst, send_sem=ss, recv_sem=rs, device_id=dev, device_id_type=MESH
        )

    bar = pltpu.get_barrier_semaphore()

    def greet(dev):
        pl.semaphore_signal(bar, inc=1, device_id=dev, device_id_type=MESH)

    key_rows = pl.ds(pl.multiple_of(core * TOK, TOK), TOK)
    loads = [
        pltpu.make_async_copy(src, dst, ld.at[i])
        for i, (src, dst) in enumerate((
            (st_ref, stb), (x_ref, xb), (gy_ref, gyb), (rate_ref, rates),
            (b_ref, bct.at[0:NST, :]), (c_ref, bct.at[NST:2 * NST, :]),
            (k_ref, kvg.at[z, key_rows, 0:HD]), (v_ref, kvg.at[z, key_rows, HD:2 * HD]),
        ))
    ]
    loads[4].start()
    loads[5].start()
    greet({"grp": (g + 4) % 8})
    for k in (4, 3, 5, 2, 6, 1, 7):
        greet({"ctx": ((z + k) % NZ) * PLANE + p})
    for k in range(1, 4):
        greet({"grp": gz + (y + k) % 4})
    for k in range(1, PLANE):
        greet({"ctx": base + plane_peer(k)})
    for load in loads[0:4] + loads[6:8]:
        load.start()

    loads[4].wait()
    loads[5].wait()
    exact = bct[...]
    tmp[...] = jnp.zeros_like(tmp)
    for i in range(3):
        piece = exact.astype(BF16).astype(F32)
        tmp[2 * NST * i:2 * NST * (i + 1), :] = piece
        exact = exact - piece
    spr[...] = tmp[...].T
    own_state = (
        lax.broadcasted_iota(jnp.int32, (NST, 128), 1) % NST
        == lax.broadcasted_iota(jnp.int32, (NST, 128), 0)
    )
    pick = jnp.where(
        (lax.broadcasted_iota(jnp.int32, (128, 256), 0) // NST) % 2
        == lax.broadcasted_iota(jnp.int32, (128, 256), 1) // 128,
        1.0, 0.0,
    ).astype(BF16)

    def spread(i, _):
        rows = [
            jnp.where(own_state, jnp.broadcast_to(spr[pl.ds(8 * i + j, 1), :], (NST, 128)), 0.0)
            for j in range(8)
        ]
        both = dot(jnp.concatenate(rows, axis=0).astype(BF16), pick, ((1,), (0,)))
        at = pl.ds(pl.multiple_of(8 * i * NST, 8 * NST), 8 * NST)
        bb[at, :] = both[:, 0:128]
        cb[at, :] = both[:, 128:256]
        return 0

    lax.fori_loop(0, TOK // 8, spread, 0, unroll=4)
    for load in loads[0:4]:
        load.wait()
    stf[...] = stb[...].astype(F32)
    uf[...] = stf[...] * xb[...].astype(F32)
    gyf[...] = gyb[...].astype(F32)
    ratel[...] = rates[...] * (-LOG2E)
    def put_total(ref, row):
        for i in range(slice_w // 128):
            ref[i:i + 1, :] = row[:, i * 128:(i + 1) * 128]

    def get_total(ref):
        return jnp.concatenate([ref[i:i + 1, :] for i in range(slice_w // 128)], axis=1)

    earlier = jnp.where(
        lax.broadcasted_iota(jnp.int32, (TOK + 8, TOK), 0)
        > lax.broadcasted_iota(jnp.int32, (TOK + 8, TOK), 1),
        1.0, 0.0,
    ).astype(BF16)

    def first_chunk(ch, _):
        lanes = pl.ds(pl.multiple_of(ch * CW, CW), CW)
        rt = ratel[:, lanes]

        def body(i, carry):
            h, pr, gg = carry
            for j in range(8):
                t = 8 * i + j
                at = pl.ds(pl.multiple_of(t * NST, NST), NST)
                bt = jnp.tile(bb[at, :], (1, CW // 128))
                ct = jnp.tile(cb[at, :], (1, CW // 128))
                a = jnp.exp2(rt * stf[pl.ds(t, 1), lanes])
                avs[at, lanes] = a
                h = a * h + uf[pl.ds(t, 1), lanes] * bt
                hs[pl.ds(pl.multiple_of((t + 1) * NST, NST), NST), lanes] = h
                pr = a * pr
                gg = gg + pr * (gyf[pl.ds(t, 1), lanes] * ct)
            return (h, pr, gg)

        zero = jnp.zeros((NST, CW), F32)
        hs[0:NST, lanes] = zero
        h, pr, gg = lax.fori_loop(0, TOK // 8, body, (zero, jnp.ones((NST, CW), F32), zero))
        before = dot(earlier, stb[:, lanes], ((1,), (0,)))
        total = before[TOK:TOK + 1, :]
        cum[:, lanes] = before
        for half in range(CW // slice_w):
            to = ch * (CW // slice_w) + half
            cut = slice(half * slice_w, (half + 1) * slice_w)
            ebuf[to, 0:NST, :] = h[:, cut].astype(BF16)
            ebuf[to, NST:2 * NST, :] = gg[:, cut].astype(BF16)
            put_total(etot.at[to], total[:, cut])
        return 0

    lax.fori_loop(0, 1, first_chunk, 0)
    loads[6].wait()
    loads[7].wait()

    pl.semaphore_wait(bar, PLANE - 1 + NZ - 1 + 3 + 1)

    def q_copy(k, whole, gathered, ss, rs):
        dst = plane_peer(k)
        cols = pl.ds(pl.multiple_of((dst % 2) * 2 * HD, 2 * HD), 2 * HD)
        rows = pl.ds(pl.multiple_of(p * TOK, TOK), TOK)
        return rcopy(
            whole.at[:, cols], gathered.at[rows, :], ss.at[k], rs.at[k], {"ctx": base + dst}
        )

    def kv_part(slot, piece):
        at = core * TOK + piece * KV_ROWS
        return kvg.at[slot, pl.ds(pl.multiple_of(at, KV_ROWS), KV_ROWS), :]

    def kv_up(s, slot, piece):
        part = kv_part(slot, piece)
        return rcopy(part, part, kz_ss.at[s, piece], kz_rs.at[s + 1, piece], {"ctx": c + PLANE})

    def kv_far(piece):
        part = kv_part(z, piece)
        return rcopy(
            part, part, kf_ss.at[piece], kz_rs.at[FAR, piece], {"ctx": c + FAR * PLANE}
        )

    def kv_over(s, slot):
        part = kvg.at[slot, pl.ds(pl.multiple_of(core * TOK, TOK), TOK), :]
        return rcopy(part, part, ks_ss.at[s], ks_rs.at[s], {"ctx": sib})

    def kv_step(s):
        slot = z - s

        @pl.when(slot >= 0)
        def _():
            for piece in range(TOK // KV_ROWS):
                @pl.when(s > 0)
                def _():
                    part = kv_part(slot, piece)
                    rcopy(
                        part, part, kz_ss.at[s, piece], kz_rs.at[s, piece], {"ctx": sib}
                    ).wait_recv()

                @pl.when(jnp.logical_and(z < NZ - 1, s != FAR - 1))
                def _():
                    kv_up(s, slot, piece).start()

            kv_over(s, slot).start()

    def kv_sib_wait(s):
        part = kvg.at[z - s, pl.ds(pl.multiple_of((1 - core) * TOK, TOK), TOK), :]
        rcopy(part, part, ks_ss.at[s], ks_rs.at[s], {"ctx": sib}).wait_recv()

    kv_step(jnp.int32(0))

    for k in FIRST_FAR:
        q_copy(k, q_ref, qg, q_ss, q_rs).start()
    my_cols = pl.ds(pl.multiple_of(core * 2 * HD, 2 * HD), 2 * HD)
    my_rows = pl.ds(pl.multiple_of(p * TOK, TOK), TOK)
    loc_q = pltpu.make_async_copy(q_ref.at[:, my_cols], qg.at[my_rows, :], loc.at[0])
    loc_do = pltpu.make_async_copy(do_ref.at[:, my_cols], dog.at[my_rows, :], loc.at[1])
    loc_q.start()
    loc_do.start()

    def first_step(ch, _):
        first_chunk(ch, 0)

        @pl.when(jnp.logical_and(ch == 1, z < NZ - FAR))
        def _():
            for piece in range(TOK // KV_ROWS):
                kv_far(piece).start()

        @pl.when(ch == 2)
        def _():
            kv_step(jnp.int32(1))

        return 0

    lax.fori_loop(1, n_chunks, first_step, 0)

    def e_copy(k):
        dst = plane_peer(k)
        return rcopy(ebuf.at[dst], erecv.at[p], ea_ss.at[k], ea_rs.at[k], {"ctx": base + dst})

    def et_copy(k):
        dst = plane_peer(k)
        return rcopy(etot.at[dst], ertot.at[p], et_ss.at[k], et_rs.at[k], {"ctx": base + dst})

    for k in FIRST_FAR:
        e_copy(k).start()
        et_copy(k).start()
    for k in FIRST_FAR:
        q_copy(k, do_ref, dog, do_ss, do_rs).start()
    erecv[p] = ebuf[p]
    ertot[p] = etot[p]

    mst[...] = jnp.full(mst.shape, NEG, F32)
    lst[...] = jnp.zeros_like(lst)
    rst[...] = jnp.zeros_like(rst)

    def tile_of(ch):
        head = ch // (1024 // ROWS)
        rows = pl.ds(pl.multiple_of((ch % (1024 // ROWS)) * ROWS, ROWS), ROWS)
        cols = pl.ds(pl.multiple_of(head * HD, HD), HD)
        lanes = pl.ds(pl.multiple_of(ch * ROWS, ROWS), ROWS)
        return rows, cols, lanes

    def seen(ch):
        key = xx * 2 * TOK + lax.broadcasted_iota(jnp.int32, (2 * TOK, ROWS), 0)
        query = (ch % (1024 // ROWS)) * ROWS + lax.broadcasted_iota(jnp.int32, (2 * TOK, ROWS), 1)
        return key <= query

    def attn_first(slot, diagonal):
        def body(ch, _):
            rows, cols, lanes = tile_of(ch)
            sc = dot(kvg[slot, :, 0:HD], qg[rows, cols], ((1,), (1,))) * (SCALE * LOG2E)
            if diagonal:
                sc = jnp.where(seen(ch), sc, NEG)
            sc = sc.reshape(2 * TOK // 8, 8, ROWS)
            dp = dot(kvg[slot, :, HD:2 * HD], dog[rows, cols], ((1,), (1,)))
            dp = dp.reshape(2 * TOK // 8, 8, ROWS)
            m_old = mst[:, lanes]
            m_new = jnp.maximum(m_old, jnp.max(sc, axis=0))
            shrink = jnp.exp2(m_old - m_new)
            pr = jnp.exp2(sc - m_new[None])
            mst[:, lanes] = m_new
            lst[:, lanes] = lst[:, lanes] * shrink + jnp.sum(pr, axis=0)
            rst[:, lanes] = rst[:, lanes] * shrink + jnp.sum(pr * dp, axis=0)
            return 0

        lax.fori_loop(0, 2 * 1024 // ROWS, body, 0, unroll=True)

    kv_step(jnp.int32(2))
    kv_step(jnp.int32(4))
    kv_step(jnp.int32(3))

    for k in range(1, PLANE):
        e_copy(k).wait()
        et_copy(k).wait()
    kv_step(jnp.int32(5))
    mine = pl.ds(pl.multiple_of(p * slice_w, slice_w), slice_w)
    rslice = ratel[:, mine]
    zero_s = jnp.zeros((NST, slice_w), F32)
    state = zero_s
    total = jnp.zeros((1, slice_w), F32)
    for j in range(PLANE):
        pre_f[j, 0:NST, :] = state
        pre_f[j, NST:2 * NST, :] = jnp.exp2(rslice * total)
        tj = get_total(ertot.at[j])
        state = jnp.exp2(rslice * tj) * state + erecv[j, 0:NST, :].astype(F32)
        total = total + tj
    plane_total = total
    zmsg_up[...] = state.astype(BF16)
    put_total(ztot, plane_total)
    state = zero_s
    total = jnp.zeros((1, slice_w), F32)
    for j in range(PLANE - 1, -1, -1):
        pre_b[j, 0:NST, :] = state
        pre_b[j, NST:2 * NST, :] = jnp.exp2(rslice * total)
        tj = get_total(ertot.at[j])
        state = jnp.exp2(rslice * tj) * state + erecv[j, NST:2 * NST, :].astype(F32)
        total = total + tj
    zmsg_dn[...] = state.astype(BF16)

    def up_copy(k):
        return rcopy(
            zmsg_up, zrecv_up.at[k], eu_ss.at[k], eu_rs.at[k], {"ctx": c + k * PLANE}
        )

    def dn_copy(k):
        return rcopy(
            zmsg_dn, zrecv_dn.at[k], ed_ss.at[k], ed_rs.at[k], {"ctx": c - k * PLANE}
        )

    def upt_copy(k):
        return rcopy(ztot, ztr_up.at[k], ut_ss.at[k], ut_rs.at[k], {"ctx": c + k * PLANE})

    def dnt_copy(k):
        return rcopy(ztot, ztr_dn.at[k], dt_ss.at[k], dt_rs.at[k], {"ctx": c - k * PLANE})

    for k in range(1, NZ):
        @pl.when(z + k < NZ)
        def _(k=k):
            upt_copy(k).start()
            up_copy(k).start()

        @pl.when(z - k >= 0)
        def _(k=k):
            dnt_copy(k).start()
            dn_copy(k).start()

    for k in range(1, PLANE):
        q_copy(k, q_ref, qg, q_ss, q_rs).wait()
        q_copy(k, do_ref, dog, do_ss, do_rs).wait()
    loc_q.wait()
    loc_do.wait()
    kv_sib_wait(jnp.int32(0))
    attn_first(z, True)
    kv_step(jnp.int32(6))

    def attn_step(s, _):
        kv_sib_wait(s)
        attn_first(z - s, False)

        @pl.when(s == 5)
        def _():
            kv_step(jnp.int32(7))

        return 0

    near = jnp.minimum(z, 3)
    lax.fori_loop(1, near + 1, attn_step, 0)

    sin_f[...] = zero_s
    sin_b[...] = zero_s
    for k in range(NZ - 1, 0, -1):
        @pl.when(z - k >= 0)
        def _(k=k):
            rcopy(
                zmsg_up, zrecv_up.at[k], eu_ss.at[k], eu_rs.at[k], {"ctx": sib}
            ).wait_recv()
            rcopy(ztot, ztr_up.at[k], ut_ss.at[k], ut_rs.at[k], {"ctx": sib}).wait_recv()
            dec = jnp.exp2(rslice * get_total(ztr_up.at[k]))
            sin_f[...] = dec * sin_f[...] + zrecv_up[k].astype(F32)

        @pl.when(z + k < NZ)
        def _(k=k):
            rcopy(
                zmsg_dn, zrecv_dn.at[k], ed_ss.at[k], ed_rs.at[k], {"ctx": sib}
            ).wait_recv()
            rcopy(ztot, ztr_dn.at[k], dt_ss.at[k], dt_rs.at[k], {"ctx": sib}).wait_recv()
            dec = jnp.exp2(rslice * get_total(ztr_dn.at[k]))
            sin_b[...] = dec * sin_b[...] + zrecv_dn[k].astype(F32)
    for j in range(PLANE):
        cbuf[j, 0:NST, :] = (
            pre_f[j, 0:NST, :] + pre_f[j, NST:2 * NST, :] * sin_f[...]
        ).astype(BF16)
        cbuf[j, NST:2 * NST, :] = (
            pre_b[j, 0:NST, :] + pre_b[j, NST:2 * NST, :] * sin_b[...]
        ).astype(BF16)

    def c_copy(k):
        dst = plane_peer(k)
        return rcopy(cbuf.at[dst], crecv.at[p], ec_ss.at[k], ec_rs.at[k], {"ctx": base + dst})

    for k in FIRST_FAR:
        c_copy(k).start()
    crecv[p] = cbuf[p]

    lax.fori_loop(near + 1, z + 1, attn_step, 0)

    m8 = mst[...]
    m1 = jnp.max(m8, axis=0, keepdims=True)
    w8 = jnp.exp2(m8 - m1)
    l1 = jnp.sum(lst[...] * w8, axis=0, keepdims=True)
    r1 = jnp.sum(rst[...] * w8, axis=0, keepdims=True)
    n_rt = 2 * 1024 // 128
    for j in range(n_rt):
        cut = slice(j * 128, (j + 1) * 128)
        stat[0, j:j + 1, :] = m1[:, cut]
        stat[0, n_rt + j:n_rt + j + 1, :] = l1[:, cut]
        stat[0, 2 * n_rt + j:2 * n_rt + j + 1, :] = r1[:, cut]

    def stat_copy(k):
        dst = base + ((xx + k) % 4) * 2 + core
        return rcopy(stat.at[0], stat.at[k], sx_ss.at[k], sx_rs.at[k], {"ctx": dst})

    for k in range(1, 4):
        stat_copy(k).start()

    def second_chunk(ch, _):
        lanes = pl.ds(pl.multiple_of(ch * CW, CW), CW)
        rt = ratel[:, lanes]
        per = CW // slice_w
        h_in = jnp.concatenate([crecv[ch * per + i, 0:NST, :] for i in range(per)], axis=1).astype(F32)
        g_in = jnp.concatenate([crecv[ch * per + i, NST:2 * NST, :] for i in range(per)], axis=1).astype(F32)
        h_end = hs[TOK * NST:(TOK + 1) * NST, lanes] + jnp.exp2(
            rt * cum[TOK:TOK + 1, lanes]
        ) * h_in

        def folded(v):
            out = v[:, 0:128]
            for i in range(1, CW // 128):
                out = out + v[:, i * 128:(i + 1) * 128]
            return out

        def backward(i, both):
            carry, h_now = both
            lo = TOK // 8 - 1 - i
            for j in range(7, -1, -1):
                t = 8 * lo + j
                at = pl.ds(pl.multiple_of(t * NST, NST), NST)
                bt = jnp.tile(bb[at, :], (1, CW // 128))
                ct = jnp.tile(cb[at, :], (1, CW // 128))
                gyt = gyf[pl.ds(t, 1), lanes]
                gn = ct * gyt + carry
                carry = avs[at, lanes] * gn
                h_before = hs[at, lanes] + jnp.exp2(rt * cum[pl.ds(t, 1), lanes]) * h_in
                qv = carry * rt * h_before
                gb = gn * bt
                for v in range(CW // 128):
                    cut = slice(v * 128, (v + 1) * 128)
                    sg[v, j * 8:(j + 1) * 8, :] = gb[0:8, cut] + gb[8:16, cut]
                    sq[v, j * 8:(j + 1) * 8, :] = qv[0:8, cut] + qv[8:16, cut]
                wacc[at, :] += folded(gn * uf[pl.ds(t, 1), lanes])
                racc[at, :] += folded(h_now * gyt)
                h_now = h_before
            rows = pl.ds(pl.multiple_of(8 * lo, 8), 8)
            for v in range(CW // 128):
                cut = slice(v * 128, (v + 1) * 128)
                a1 = sg[v, pl.ds(0, 8, stride=8), :]
                a2 = sq[v, pl.ds(0, 8, stride=8), :]
                for n in range(1, 8):
                    a1 = a1 + sg[v, pl.ds(n, 8, stride=8), :]
                    a2 = a2 + sq[v, pl.ds(n, 8, stride=8), :]
                s1[rows, cut] = a1
                s2[rows, cut] = a2
            return carry, h_now

        lax.fori_loop(0, TOK // 8, backward, (g_in, h_end), unroll=2)
        gxb[:, lanes] = (s1[...] * stf[:, lanes]).astype(BF16)
        gsb[:, lanes] = (
            s1[...] * xb[:, lanes].astype(F32) + LN2 * s2[...]
        ).astype(BF16)
        return 0

    def y_copy(k):
        return rcopy(wred, yrecv.at[k], y_ss.at[k], y_rs.at[k], {"grp": gz + (y + k) % 4})

    h_copy = rcopy(hsum, hrecv, hh_ss, hh_rs, {"grp": (g + 4) % 8})

    def states_here():
        for k in range(1, PLANE):
            c_copy(k).wait()
        wacc[...] = jnp.zeros_like(wacc)
        racc[...] = jnp.zeros_like(racc)

    gx_out = pltpu.make_async_copy(gxb, gx_ref, loc.at[5])
    gs_out = pltpu.make_async_copy(gsb, gs_ref, loc.at[6])

    def coefficients():
        gx_out.start()
        gs_out.start()
        ones = jnp.ones((8, 256), BF16)
        for n in range(NST):
            for acc, to in ((wacc, n), (racc, NST + n)):
                part = acc[pl.ds(n, TOK, stride=NST), :]
                high = part.astype(BF16)
                low = (part - high.astype(F32)).astype(BF16)
                total = dot(ones, jnp.concatenate([high, low], axis=1), ((1,), (1,)))
                wred[to:to + 1, :] = total[0:1, :]

        for k in range(1, 4):
            y_copy(k).start()

    def across_z_hi():
        for k in range(1, 4):
            y_copy(k).wait()
        hsum[...] = wred[...] + yrecv[1] + yrecv[2] + yrecv[3]
        h_copy.start()

    def all_stats():
        for k in range(1, 4):
            stat_copy(k).wait()
        m4 = [stat[k, 0:n_rt, :] for k in range(4)]
        m_all = jnp.maximum(jnp.maximum(m4[0], m4[1]), jnp.maximum(m4[2], m4[3]))
        l_all = jnp.zeros((n_rt, 128), F32)
        r_all = jnp.zeros((n_rt, 128), F32)
        for k in range(4):
            w = jnp.exp2(m4[k] - m_all)
            l_all = l_all + w * stat[k, n_rt:2 * n_rt, :]
            r_all = r_all + w * stat[k, 2 * n_rt:3 * n_rt, :]
        lse_t = m_all + jnp.log2(l_all)
        rd_t = r_all / l_all
        for j in range(n_rt):
            cut = slice(j * 128, (j + 1) * 128)
            lse[:, cut] = jnp.broadcast_to(lse_t[j:j + 1, :], (8, 128))
            rdt[:, cut] = jnp.broadcast_to(rd_t[j:j + 1, :], (8, 128))

    dqt[...] = jnp.zeros_like(dqt)

    def dq_to(dst):
        cols = slice(dst * TOK, (dst + 1) * TOK)
        return rcopy(
            dqs.at[:, cols], dqr.at[p], dq_ss.at[dst], dq_rs.at[p], {"ctx": base + dst}
        )

    def dq_from(src):
        return rcopy(
            dqs.at[:, 0:TOK], dqr.at[src], dq_ss.at[src], dq_rs.at[src], {"ctx": base + src}
        )

    def dq_leave(first, last):
        cols = slice(first * TOK, last * TOK)
        dqs[:, cols] = (dqt[:, cols] * SCALE).astype(BF16)
        for dst in range(first, last):
            @pl.when(p != dst)
            def _(dst=dst):
                dq_to(dst).start()

            @pl.when(p == dst)
            def _(dst=dst):
                dqr[dst] = dqs[:, dst * TOK:(dst + 1) * TOK]

    def attn_second(s, slot, diagonal):
        keys_t = kvg[slot, :, 0:HD].T

        def body(ch, carry):
            dk, dv = carry
            rows, cols, lanes = tile_of(ch)
            keys = kvg[slot, :, 0:HD]
            sc = dot(keys, qg[rows, cols], ((1,), (1,))) * (SCALE * LOG2E)
            pr = jnp.exp2(sc.reshape(2 * TOK // 8, 8, ROWS) - lse[:, lanes][None])
            if diagonal:
                pr = jnp.where(seen(ch).reshape(pr.shape), pr, 0.0)
            dp = dot(kvg[slot, :, HD:2 * HD], dog[rows, cols], ((1,), (1,)))
            ds = pr * (dp.reshape(pr.shape) - rdt[:, lanes][None])
            pb = pr.reshape(2 * TOK, ROWS).astype(BF16)
            db = ds.reshape(2 * TOK, ROWS).astype(BF16)
            dv = dv + dot(pb, dog[rows, cols], ((1,), (0,)))
            dk = dk + dot(db, qg[rows, cols], ((1,), (0,)))
            head = pl.ds(pl.multiple_of((ch // (1024 // ROWS)) * HD, HD), HD)
            dqt[head, rows] += dot(keys_t, db, ((1,), (0,)))
            return dk, dv

        zero = jnp.zeros((2 * TOK, HD), F32)
        if diagonal:
            both = (zero, zero)
            per_head = 1024 // ROWS
            for part in range(per_head):
                for head in range(2):
                    both = body(jnp.int32(head * per_head + part), both)
                dq_leave(part * PLANE // per_head, (part + 1) * PLANE // per_head)
            dk, dv = both
        else:
            dk, dv = lax.fori_loop(0, 2 * 1024 // ROWS, body, (zero, zero), unroll=True)
        dk = dk * SCALE
        first = core == 0
        own[s, :, 0:HD] = jnp.where(first, dk[0:TOK], dk[TOK:])
        own[s, :, HD:2 * HD] = jnp.where(first, dv[0:TOK], dv[TOK:])
        sib_s[s, :, 0:HD] = jnp.where(first, dk[TOK:], dk[0:TOK])
        sib_s[s, :, HD:2 * HD] = jnp.where(first, dv[TOK:], dv[0:TOK])
        sib_copy(s).start()

    def sib_copy(s):
        return rcopy(sib_s.at[s], sib_r.at[s], si_ss.at[s], si_rs.at[s], {"ctx": sib})

    def z_copy(s):
        return rcopy(
            zs.at[s], zr.at[s], zz_ss.at[s], zz_rs.at[s], {"ctx": c - s * PLANE}
        )

    def hand_down(s):
        sib_copy(s).wait()
        zs[s] = (own[s] + sib_r[s]).astype(BF16)
        z_copy(s).start()

    turn = jnp.maximum(z - 2, 0)

    def second_step(i, _):
        s = z - i

        @pl.when(i == 0)
        def _():
            states_here()

        @pl.when(jnp.logical_or(i == 0, i == turn))
        def _():
            first = jnp.where(i == 0, 0, 1)
            last = jnp.where(i == turn, n_chunks, 1)
            lax.fori_loop(first, last, second_chunk, 0)

        @pl.when(jnp.logical_and(i > 0, i == turn))
        def _():
            hand_down(s + 1)

        @pl.when(i == turn)
        def _():
            coefficients()

        @pl.when(i == 0)
        def _():
            all_stats()

        @pl.when(i < z)
        def _():
            attn_second(s, z - s, False)

        @pl.when(i == z)
        def _():
            attn_second(jnp.int32(0), z, True)

        @pl.when(jnp.logical_and(i > 0, i != turn))
        def _():
            hand_down(s + 1)

        @pl.when(i == jnp.minimum(turn + 2, z))
        def _():
            across_z_hi()

        return 0

    lax.fori_loop(0, z + 1, second_step, 0)

    sib_copy(jnp.int32(0)).wait()

    for other in range(PLANE):
        @pl.when(p != other)
        def _(other=other):
            dq_to(other).wait_send()
            dq_from(other).wait_recv()

    for cc in range(2):
        tot = dqr[cc].astype(F32)
        for i in range(1, 4):
            tot = tot + dqr[2 * i + cc].astype(F32)
        for h in range(2):
            col = (cc * 2 + h) * HD
            dq_ref[:, col:col + HD] = tot[h * HD:(h + 1) * HD, :].T.astype(BF16)

    own[0] = own[0] + sib_r[0]
    for k in range(1, NZ):
        @pl.when(z + k < NZ)
        def _(k=k):
            rcopy(zs.at[k], zr.at[k], zz_ss.at[k], zz_rs.at[k], {"ctx": sib}).wait_recv()
            own[0] = own[0] + zr[k].astype(F32)
    dk_ref[...] = own[0, :, 0:HD].astype(BF16)
    dv_ref[...] = own[0, :, HD:2 * HD].astype(BF16)

    gx_out.wait()
    gs_out.wait()
    h_copy.wait()
    gw_ref[...] = hsum[0:NST, :] + hrecv[0:NST, :]
    gr_ref[...] = hsum[NST:2 * NST, :] + hrecv[NST:2 * NST, :]

    for k in range(1, NZ):
        @pl.when(z + k < NZ)
        def _(k=k):
            up_copy(k).wait_send()
            upt_copy(k).wait_send()

        @pl.when(z - k >= 0)
        def _(k=k):
            dn_copy(k).wait_send()
            dnt_copy(k).wait_send()
            z_copy(k).wait_send()
    for s in range(NZ):
        @pl.when(z - s >= 0)
        def _(s=s):
            kv_over(s, z - s).wait_send()

            if s != FAR - 1:
                @pl.when(z < NZ - 1)
                def _():
                    for piece in range(TOK // KV_ROWS):
                        kv_up(s, z - s, piece).wait_send()

    @pl.when(z < NZ - FAR)
    def _():
        for piece in range(TOK // KV_ROWS):
            kv_far(piece).wait_send()


def hand_over(*refs):
    copies = [pltpu.make_async_copy(refs[i], refs[7 + i], refs[14].at[i]) for i in range(7)]
    for copy in copies:
        copy.start()
    for copy in copies:
        copy.wait()


def on_device(
    queries, key_vectors, value_vectors, grad_attn, mamba_input, step_sizes, decay_rates,
    write_coef, read_coef, grad_mamba,
):
    channels = mamba_input.shape[1]
    slice_w = channels // PLANE
    vmem = pltpu.VMEM
    dma = pltpu.SemaphoreType.DMA
    scratch = [
        vmem((TOK, channels), BF16), vmem((TOK, channels), BF16),
        vmem((TOK, channels), BF16), vmem((TOK, channels), BF16), vmem((TOK, channels), BF16),
        vmem((NST, channels), F32), vmem((2 * NST, TOK), F32), vmem((128, 128), F32),
        vmem((1024, 256), BF16), vmem((1024, 256), BF16), vmem((NZ, 256, 256), BF16),
        vmem((TOK, channels), F32), vmem((TOK, channels), F32), vmem((TOK, channels), F32),
        vmem((TOK * NST, 128), F32), vmem((TOK * NST, 128), F32), vmem((128, 128), F32),
        vmem((NST, channels), F32),
        vmem((PLANE, 32, slice_w), BF16), vmem((PLANE, 32, slice_w), BF16),
        vmem((NST, slice_w), BF16), vmem((NST, slice_w), BF16),
        vmem((NZ, NST, slice_w), BF16), vmem((NZ, NST, slice_w), BF16),
        vmem((PLANE, 32, slice_w), F32), vmem((PLANE, 32, slice_w), F32),
        vmem((NST, slice_w), F32), vmem((NST, slice_w), F32),
        vmem((PLANE, 32, slice_w), BF16), vmem((PLANE, 32, slice_w), BF16),
        vmem((8, 2048), F32), vmem((8, 2048), F32), vmem((8, 2048), F32),
        vmem((4, 48, 128), F32), vmem((8, 2048), F32), vmem((8, 2048), F32),
        vmem((256, 1024), F32), vmem((256, 1024), BF16), vmem((PLANE, 256, 128), BF16),
        vmem((NZ, 128, 256), F32), vmem((NZ, 128, 256), F32), vmem((NZ, 128, 256), F32),
        vmem((NZ, 128, 256), BF16), vmem((NZ, 128, 256), BF16),
        vmem(((TOK + 1) * NST, channels), F32), vmem((TOK * NST, channels), F32),
        vmem((TOK + 8, channels), F32),
        vmem((CW // 128, 64, 128), F32), vmem((CW // 128, 64, 128), F32), vmem((TOK, CW), F32), vmem((TOK, CW), F32),
        vmem((TOK * NST, 128), F32), vmem((TOK * NST, 128), F32),
        vmem((32, 128), F32), vmem((4, 32, 128), F32), vmem((32, 128), F32), vmem((32, 128), F32),
        dma((8,)), dma((8,)), dma((8,)), dma((8,)),
        dma((8, TOK // KV_ROWS)), dma((8, TOK // KV_ROWS)), dma((TOK // KV_ROWS,)),
        dma((8,)), dma((8,)),
        dma((8,)),
        dma((8,)), dma((8,)), dma((8,)), dma((8,)), dma((8,)), dma((8,)), dma((8,)), dma((8,)),
        dma((4,)), dma((4,)), dma((8,)), dma((8,)), dma((8,)), dma((8,)), dma((8,)), dma((8,)),
        dma((4,)), dma((4,)), dma, dma, dma((8,)),
        vmem((PLANE, slice_w // 128, 128), F32), vmem((PLANE, slice_w // 128, 128), F32),
        vmem((slice_w // 128, 128), F32),
        vmem((NZ, slice_w // 128, 128), F32), vmem((NZ, slice_w // 128, 128), F32),
        dma((8,)), dma((8,)), dma((8,)), dma((8,)), dma((8,)), dma((8,)),
    ]
    outs = (
        jax.ShapeDtypeStruct(queries.shape, BF16),
        jax.ShapeDtypeStruct(key_vectors.shape, BF16),
        jax.ShapeDtypeStruct(value_vectors.shape, BF16),
        jax.ShapeDtypeStruct(mamba_input.shape, BF16),
        jax.ShapeDtypeStruct(step_sizes.shape, BF16),
        jax.ShapeDtypeStruct((NST, TOK), F32),
        jax.ShapeDtypeStruct((NST, TOK), F32),
    )
    made = pl.pallas_call(
        kernel,
        out_shape=outs,
        in_specs=[pl.BlockSpec(memory_space=pl.ANY)] * 10,
        out_specs=(pl.BlockSpec(memory_space=pltpu.VMEM),) * 3
        + (pl.BlockSpec(memory_space=pl.ANY),) * 2
        + (pl.BlockSpec(memory_space=pltpu.VMEM),) * 2,
        scratch_shapes=scratch,
        compiler_params=pltpu.CompilerParams(
            collective_id=0, has_side_effects=True, vmem_limit_bytes=60 * 2**20
        ),
    )(
        queries, key_vectors, value_vectors, grad_attn, mamba_input, step_sizes, decay_rates,
        write_coef.T, read_coef.T, grad_mamba,
    )
    out = pl.pallas_call(
        hand_over,
        out_shape=outs,
        in_specs=[pl.BlockSpec(memory_space=pltpu.VMEM)] * 7,
        out_specs=(pl.BlockSpec(memory_space=pltpu.HBM),) * 7,
        scratch_shapes=[dma((7,))],
    )(*made)
    return out[:5] + (out[5].T, out[6].T)


def solution(mesh):
    both = P("ctx", "grp")
    rows = P("ctx", None)
    return jax.shard_map(
        on_device,
        mesh=mesh,
        in_specs=(both,) * 6 + (P(None, "grp"), rows, rows, both),
        out_specs=(both,) * 5 + (rows, rows),
        check_vma=False,
    )
```
